256 devices in a mesh: dom: 64 (over z, x, core), sub: 4 (over y).
Axes of the slice: x: 4, y: 4, z: 8, core: 2. Of those that a mesh axis runs over, the one named last changes fastest.
Arguments:
- dofs: float32 [9, 35, 32768], P(None, None, ('dom', 'sub')), may hold values from -6 to 6
- star_matrix: float32 [3, 9, 9, 32768], P(None, None, None, ('dom', 'sub')), may hold values from -2 to 2
- local_solver: float32 [4, 9, 9, 32768], P(None, None, None, ('dom', 'sub')), may hold values from -2 to 2
- neigh_solver: float32 [4, 9, 9, 32768], P(None, None, None, ('dom', 'sub')), may hold values from -2 to 2
- elem_cluster: int32 [32768], P(('dom', 'sub')), may hold values from 0 to 2, as said below
- face_nbr: int32 [4, 32768], P(None, ('dom', 'sub')), may hold values from 0 to 767, as said below
- nbr_face: int32 [4, 32768], P(None, ('dom', 'sub')), may hold values from 0 to 3
- send_table: int32 [768, 5, 4, 32], P(('dom', 'sub')), may hold values from 0 to 128, as said below
- fault_elem: int32 [8192], P(('dom', 'sub')), may hold values from 0 to 127, as said below
- fault_face: int32 [8192], P(('dom', 'sub')), may hold values from 0 to 3
- fault_coef: float32 [9, 8192], P(None, ('dom', 'sub')), may hold values from 0.1 to 0.9
- ck_matrix: float32 [3, 35, 35], replicated, may hold values from -1 to 1
- stiffness: float32 [3, 35, 35], replicated, may hold values from -0.36 to 0.36
- local_flux: float32 [4, 35, 35], replicated, may hold values from -0.36 to 0.36
- neigh_flux: float32 [4, 4, 35, 35], replicated, may hold values from -0.36 to 0.36
- face_trace: float32 [4, 15, 35], replicated, may hold values from -1 to 1
- face_lift: float32 [4, 35, 15], replicated, may hold values from -0.9 to 0.9
Outputs:
- new_dofs: float32 [9, 35, 32768], P(None, None, ('dom', 'sub'))
The draws below stay inside these ranges and needn't reach their ends.
Inputs may be any that keep to these rules, and one draw needn't show every extreme that they name: `elem_cluster`: every element named in fault_elem is in cluster 0. `face_nbr`: values below 128 name a local element of the same device; a value 128 + q names ghost slot q of the element's own cluster. `send_table`: entry [3 * device + c, r, t, k] is the k-th local element whose cluster-c integral the device sends to the device with dom index greater by r - 2 and sub index t; 128 marks an empty slot. `fault_elem`: the fault slots of one device name distinct local elements; slot k of a device and slot k of the device with the same dom index and sub index XOR 2 are the two sides of one fault face.
All inputs are finite; a program needn't handle non-finite values.
Results may differ from the reference program's by a relative error of at most 0.0001.
Values sent between devices are 32-bit elements; how exact they have to be, the bound alone decides.
A program may use at most 192 MiB of HBM per device.

```python
import math
import jax
import jax.numpy as jnp
from jax import lax

Q = 9
B = 35
FB = 15
E_DEV = 128
GSLOT = 32
FAULT_DEV = 32
ELEMS = 32768
FAULTS = 8192
N_DOM = 64
N_SUB = 4


def fault_members(key):
    key = jax.random.fold_in(key, 91)
    devices = ELEMS // E_DEV
    scores = jax.random.randint(key, (devices, E_DEV), 0, 1 << 20) * E_DEV + jnp.arange(E_DEV)[None, :]
    scores = scores.at[0, E_DEV - 1].set(-1).at[0, 0].set(-2)
    ordering = jnp.argsort(scores, axis=1)
    return ordering[:, :FAULT_DEV].astype(jnp.int32)


def draw_fault_elem(key, part):
    members = fault_members(key)
    return members.reshape(-1).astype(jnp.int32)


def draw_elem_cluster(key, part):
    members = fault_members(key)
    key = jax.random.fold_in(key, 3)
    devices = ELEMS // E_DEV
    cluster = jax.random.randint(key, (ELEMS,), 0, 3)
    glob = (jnp.arange(devices)[:, None] * E_DEV + members).reshape(-1)
    return cluster.at[glob].set(0).astype(jnp.int32)


def draw_face_nbr(key, part):
    key = jax.random.fold_in(key, 5)
    first, second, third = jax.random.split(key, 3)
    slots = 5 * N_SUB * GSLOT
    local_ids = jax.random.randint(first, (4, ELEMS), 0, E_DEV)
    ghost_ids = E_DEV + jax.random.randint(second, (4, ELEMS), 0, slots)
    chosen = jax.random.randint(third, (4, ELEMS), 0, 4) == 0
    values = jnp.where(chosen, ghost_ids, local_ids)
    values = values.at[0, ::E_DEV].set(E_DEV + slots - 1)
    return values.astype(jnp.int32)


def draw_send_table(key, part):
    key = jax.random.fold_in(key, 7)
    first, second = jax.random.split(key, 2)
    devices = ELEMS // E_DEV
    shape = (devices * 3, 5, N_SUB, GSLOT)
    fewest = max(1, GSLOT // 4)
    entries = jax.random.randint(first, shape, 0, E_DEV)
    used = jax.random.randint(second, (devices * 3, 5, N_SUB), fewest, GSLOT + 1)
    used = used.at[::3, 0, 0].set(GSLOT)
    used = used.at[::3, 1, 0].set(fewest)
    keeping = jnp.arange(GSLOT)[None, None, None, :] < used[..., None]
    return jnp.where(keeping, entries, E_DEV).astype(jnp.int32)


def set_ends(values, key, least, high):
    dims = values.shape
    spot = [jax.random.randint(jax.random.fold_in(key, axis), (), 0, dims[axis]) for axis in range(len(dims))]
    values = values.at[tuple(spot)].set(least)
    longest = dims.index(max(dims))
    spot[longest] = (spot[longest] + 1) % dims[longest]
    return values.at[tuple(spot)].set(high)


def block_scale(stream_key, extent, shards, smallest, top_value):
    def one(dim, blocks):
        heights = jax.random.uniform(jax.random.fold_in(jax.random.fold_in(stream_key, 6), dim), (blocks,), jnp.float32, smallest / len(shards), top_value / len(shards))
        return jnp.repeat(jnp.exp(heights), extent[dim] // blocks).reshape((-1,) + (1,) * (len(extent) - dim - 1))

    factor_of = one(*shards[0])
    for cut in shards[1:]:
        factor_of = factor_of * one(*cut)
    return factor_of


def noise(key, extent, spread, limit, cuts=(), held_as=jnp.bfloat16):
    values = jax.random.normal(key, extent, jnp.float32) * spread
    if len(cuts) > 0:
        values = block_scale(key, extent, cuts, -0.22, 0.18) * values
    return jnp.clip(values, min=-limit, max=limit).astype(held_as)


def setup_inputs(seed: int = 0) -> dict:
    keys = jax.random.split(jax.random.key(seed), 18)
    dofs = noise(keys[0], (Q, B, ELEMS), 1.0, 6.0, ((2, 256),), jnp.float32)
    star_matrix = noise(keys[1], (3, Q, Q, ELEMS), Q ** -0.5, 2.0, ((3, 256),), jnp.float32)
    local_solver = noise(keys[2], (4, Q, Q, ELEMS), Q ** -0.5, 2.0, ((3, 256),), jnp.float32)
    neigh_solver = noise(keys[3], (4, Q, Q, ELEMS), Q ** -0.5, 2.0, ((3, 256),), jnp.float32)
    elem_cluster = draw_elem_cluster(jax.random.fold_in(keys[17], 71), 0)
    face_nbr = draw_face_nbr(jax.random.fold_in(keys[17], 71), 0)
    nbr_face = set_ends(jax.random.randint(keys[6], (4, ELEMS), 0, 4), jax.random.fold_in(keys[6], 1), 0, 3).astype(jnp.int32)
    send_table = draw_send_table(jax.random.fold_in(keys[17], 71), 0)
    fault_elem = draw_fault_elem(jax.random.fold_in(keys[17], 71), 0)
    fault_face = set_ends(jax.random.randint(keys[9], (FAULTS,), 0, 4), jax.random.fold_in(keys[9], 1), 0, 3).astype(jnp.int32)
    fault_coef = jnp.clip(0.1 + 0.79999997 * jax.random.uniform(keys[10], (Q, FAULTS), jnp.float32) ** block_scale(keys[10], (Q, FAULTS), ((1, 256),), -0.2, 0.2), 0.1, 0.9)
    ck_matrix = noise(keys[11], (3, B, B), B ** -0.5, 1.0, (), jnp.float32)
    stiffness = noise(keys[12], (3, B, B), 0.06, 0.36, (), jnp.float32)
    local_flux = noise(keys[13], (4, B, B), 0.06, 0.36, (), jnp.float32)
    neigh_flux = noise(keys[14], (4, 4, B, B), 0.06, 0.36, (), jnp.float32)
    face_trace = noise(keys[15], (4, FB, B), B ** -0.5, 1.0, (), jnp.float32)
    face_lift = noise(keys[16], (4, B, FB), 0.15, 0.9, (), jnp.float32)
    return {"dofs": dofs, "star_matrix": star_matrix, "local_solver": local_solver, "neigh_solver": neigh_solver, "elem_cluster": elem_cluster, "face_nbr": face_nbr, "nbr_face": nbr_face, "send_table": send_table, "fault_elem": fault_elem, "fault_face": fault_face, "fault_coef": fault_coef, "ck_matrix": ck_matrix, "stiffness": stiffness, "local_flux": local_flux, "neigh_flux": neigh_flux, "face_trace": face_trace, "face_lift": face_lift}


HIGHEST_PRECISION = lax.Precision.HIGHEST
time_step = 0.25


def basis_apply(matrix, values):
    return jnp.einsum("kl,qle->qke", matrix, values, precision=HIGHEST_PRECISION)


def star_apply(matrix, values):
    summed = matrix[:, 0, None, :] * values[0][None]
    for column in range(1, values.shape[0]):
        summed = summed + matrix[:, column, None, :] * values[column][None]
    return summed


def derive(current, star_matrix, ck_matrix):
    derivs = [current]
    for degree in range(4):
        summed = jnp.zeros_like(current)
        for direction in range(3):
            summed = summed + star_apply(star_matrix[direction], basis_apply(ck_matrix[direction], derivs[-1]))
        derivs.append(-summed)
    return jnp.stack(derivs)


def integrate(derivs, offset, length):
    summed = jnp.zeros_like(derivs[0])
    for degree in range(5):
        weight = ((offset + length) ** (degree + 1) - offset ** (degree + 1)) / math.factorial(degree + 1)
        summed = summed + weight[None, None, :] * derivs[degree]
    return summed


def flux_change(own_part, neighbours, nbr_face, star_matrix, local_solver, neigh_solver, stiffness, local_flux, neigh_flux):
    change = jnp.zeros_like(own_part)
    for direction in range(3):
        change = change + star_apply(star_matrix[direction], basis_apply(stiffness[direction], own_part))
    for face_index in range(4):
        change = change - star_apply(local_solver[face_index], basis_apply(local_flux[face_index], own_part))
        lifted = jnp.zeros_like(own_part)
        for other in range(4):
            masked = jnp.where((nbr_face[face_index] == other)[None, None, :], neighbours[face_index], 0.0)
            lifted = lifted + basis_apply(neigh_flux[face_index, other], masked)
        change = change - star_apply(neigh_solver[face_index], lifted)
    return change


def reference(dofs, star_matrix, local_solver, neigh_solver, elem_cluster, face_nbr, nbr_face, send_table, fault_elem, fault_face, fault_coef, ck_matrix, stiffness, local_flux, neigh_flux, face_trace, face_lift):
    devices = N_DOM * N_SUB
    elems = dofs.shape[2]
    per_device = elems // devices
    slots = 5 * N_SUB * GSLOT
    owner = jnp.arange(elems, dtype=jnp.int32) // per_device
    table = send_table.reshape(devices, 3, 5, N_SUB, GSLOT)
    device_ids = jnp.arange(devices, dtype=jnp.int32)
    dom_index = device_ids // N_SUB
    sub_index = device_ids % N_SUB
    offsets_grid = jnp.arange(5, dtype=jnp.int32)[None, :, None]
    subs_grid = jnp.arange(N_SUB, dtype=jnp.int32)[None, None, :]
    source_dom = dom_index[:, None, None] - offsets_grid + 2
    inside = (source_dom >= 0) & (source_dom < N_DOM)
    source = jnp.clip(source_dom, 0, N_DOM - 1) * N_SUB + subs_grid
    columns = []
    for cluster in range(3):
        entries = table[source, cluster, offsets_grid, sub_index[:, None, None], :]
        ghost_cols = jnp.where(inside[..., None] & (entries < per_device), source[..., None] * per_device + entries, elems)
        ghost_flat = ghost_cols.reshape(-1).astype(jnp.int32)
        per_face = []
        for face_index in range(4):
            local_ids = face_nbr[face_index]
            ghost_pos = owner * slots + jnp.clip(local_ids - per_device, 0, slots - 1)
            per_face.append(jnp.where(local_ids < per_device, owner * per_device + local_ids, ghost_flat[ghost_pos]).astype(jnp.int32))
        columns.append(per_face)
    period = jnp.where(elem_cluster == 0, 1, jnp.where(elem_cluster == 1, 2, 4)).astype(jnp.int32)
    fault_count = fault_elem.shape[0]
    fault_glob = ((jnp.arange(fault_count, dtype=jnp.int32) // FAULT_DEV) * per_device + fault_elem).astype(jnp.int32)
    partner = jnp.bitwise_xor(device_ids, 2)
    fault_traces = face_trace[fault_face]
    fault_lifts = face_lift[fault_face]
    fault_solver = neigh_solver[fault_face, :, :, fault_glob]
    current = dofs
    derivs = None
    for substep in range(4):
        active = (substep % period) == 0
        renewed = derive(current, star_matrix, ck_matrix)
        if substep == 0:
            derivs = renewed
        else:
            derivs = jnp.where(active[None, None, None, :], renewed, derivs)
        offset = (substep % period).astype(jnp.float32) * time_step
        due_list = [cluster for cluster in range(3) if substep % (2 ** cluster) == 0]
        own_part = jnp.zeros_like(current)
        neighbours = [jnp.zeros_like(current) for face_index in range(4)]
        integral_zero = None
        for cluster in due_list:
            integral = integrate(derivs, offset, time_step * 2 ** cluster)
            if cluster == 0:
                integral_zero = integral
            member = (elem_cluster == cluster)[None, None, :]
            own_part = jnp.where(member, integral, own_part)
            padded = jnp.concatenate([integral, jnp.zeros((integral.shape[0], integral.shape[1], 1), jnp.float32)], axis=2)
            for face_index in range(4):
                fetched = jnp.take(padded, columns[cluster][face_index], axis=2)
                neighbours[face_index] = jnp.where(member, fetched, neighbours[face_index])
        change = flux_change(own_part, neighbours, nbr_face, star_matrix, local_solver, neigh_solver, stiffness, local_flux, neigh_flux)
        near_side = jnp.einsum("fml,qlf->qmf", fault_traces, integral_zero[:, :, fault_glob], precision=HIGHEST_PRECISION)
        far_side = near_side.reshape(near_side.shape[0], near_side.shape[1], devices, FAULT_DEV)[:, :, partner, :].reshape(near_side.shape)
        fault_state = 0.5 * (near_side + far_side) + fault_coef[:, None, :] * (far_side - near_side)
        lifted = jnp.einsum("flm,qmf->qlf", fault_lifts, fault_state, precision=HIGHEST_PRECISION)
        contrib = jnp.einsum("fpq,qlf->plf", fault_solver, lifted, precision=HIGHEST_PRECISION)
        change = change - jnp.zeros_like(current).at[:, :, fault_glob].add(contrib)
        current = current + jnp.where(active[None, None, :], change, 0.0)
    return current
```

```python
import functools

import jax
import jax.numpy as jnp
from jax import lax
from jax.experimental import pallas as pl
from jax.experimental.pallas import tpu as pltpu
from jax.sharding import PartitionSpec as P

MESH = pl.DeviceIdType.MESH
F32 = jnp.float32
BF16 = jnp.bfloat16
Q = 9
B = 35
KP = 40
E = 128
W = Q * E
FB = 15
NF = 32
SLOT = 32
REACH = 5
N_SUB = 4
PEERS = REACH * N_SUB
ROWS = 320
PIECE = ROWS // N_SUB
TAIL = Q * 32
STEP = 0.25
ROUTES = {(0, 0): 0, (0, 1): 1, (0, 2): 2, (1, 0): 3, (2, 0): 4, (2, 1): 5, (3, 0): 6}


def halves(value):
    high = value.astype(BF16).astype(F32)
    return high, value - high


def stacked(value):
    high, low = halves(value)
    return jnp.concatenate([high, low, high, jnp.zeros((8, E), F32)], axis=0).astype(BF16)


def weights(matrix, width):
    high, low = halves(matrix)
    return high + pltpu.roll(high, width, 1) + pltpu.roll(low, 2 * width, 1)


def dot(left, right):
    return jnp.dot(left, right, preferred_element_type=F32)


def lanes(index, count=1):
    return pl.ds(pl.multiple_of(index * E, E), count * E)


def exchanged(parts, low_half, even):
    mixed = [None] * 4
    for g in range(2):
        mixed[g] = jnp.where(low_half, parts[g], pltpu.roll(parts[g + 2], 64, 1))
        mixed[g + 2] = jnp.where(low_half, pltpu.roll(parts[g], 64, 1), parts[g + 2])
    out = [None] * 4
    for g in (0, 2):
        out[g] = jnp.where(even, mixed[g], pltpu.roll(mixed[g + 1], 32, 1))
        out[g + 1] = jnp.where(even, pltpu.roll(mixed[g], 96, 1), mixed[g + 1])
    return out


def kernel(
    n_dom,
    dofs,
    star,
    lsol,
    nsol,
    ecl,
    fnbr,
    nface,
    stab,
    felem,
    fface,
    fcoef,
    ck,
    stiff,
    lflux,
    nflux,
    ftrace,
    flift,
    out,
    base,
    cur,
    integ,
    x_der,
    x_own,
    x_nbr,
    x_state,
    moved,
    across,
    lifted,
    lift,
    near,
    far,
    fsend,
    frecv,
    comp,
    comp_h,
    got,
    ghost,
    packed,
    pick,
    pick_send,
    pick_f,
    pick_ft,
    a_ck,
    a_vol,
    a_nf,
    a_tr,
    a_li,
    wide,
    tab,
    fer,
    cfs,
    cfe,
    wt,
    send,
    recv,
    send_sem,
    recv_sem,
    fsend_sem,
    frecv_sem,
):
    dom = lax.axis_index("dom")
    sub = lax.axis_index("sub")

    def out_peer(idx):
        r, t = idx // N_SUB, idx % N_SUB
        peer = dom + r - 2
        valid = (peer >= 0) & (peer < n_dom) & jnp.logical_not((r == 2) & (t == sub))
        return peer, t, valid

    def in_peer(idx):
        r, t = idx // N_SUB, idx % N_SUB
        peer = dom - r + 2
        valid = (peer >= 0) & (peer < n_dom) & jnp.logical_not((r == 2) & (t == sub))
        return peer, t, valid

    barrier = pltpu.get_barrier_semaphore()

    @pl.loop(0, PEERS)
    def _(idx):
        peer, t, valid = out_peer(idx)

        @pl.when(valid)
        def _():
            pl.semaphore_signal(barrier, inc=1, device_id=(peer, t), device_id_type=MESH)

    lane = lax.broadcasted_iota(jnp.int32, (16, E), 1)
    low_half = lane < 64
    even = (lane // 32) % 2 == 0
    element_rows = lax.broadcasted_iota(jnp.int32, (E, E), 0)

    base[...] = jnp.zeros((Q, KP, E), F32)
    base[:, :B, :] = dofs[...]
    cur[...] = base[...]
    wide[...] = jnp.zeros(wide.shape, F32)
    for d in range(3):
        wide[d, :B, :B] = ck[d]
    a_ck[...] = jnp.concatenate(
        [weights(wide[d], KP) for d in range(3)] + [jnp.zeros((8, E), F32)], axis=0
    ).astype(BF16)
    cluster_of = ecl[...]

    def star_terms(acc, coef, first, rows, group, sign):
        for q in range(Q):
            value = moved[rows : rows + KP, q * E : (q + 1) * E]
            for pp in range(3):
                term = coef[first, group * 3 + pp, q : q + 1, :] * value
                if acc[pp] is None:
                    acc[pp] = term if sign > 0 else -term
                else:
                    acc[pp] = acc[pp] + term if sign > 0 else acc[pp] - term
        return acc

    def derive(s, due):
        if s > 0:
            keep = cluster_of == 0
            if s % 2 == 0:
                keep = cluster_of <= 1
            for q in range(Q):
                base[q] = jnp.where(keep, cur[q], base[q])
        offset = jnp.where(
            cluster_of == 0, 0.0, jnp.where(cluster_of == 1, (s % 2) * STEP, (s % 4) * STEP)
        ).astype(F32)
        for c in due:
            end = offset + STEP * 2**c
            upper, lower, factor = end, offset, 1.0
            for j in range(5):
                factor = factor * (j + 1)
                wt[5 * c + j : 5 * c + j + 1, :] = (upper - lower) * (1.0 / factor)
                upper, lower = upper * end, lower * offset
        for q in range(Q):
            value = base[q]
            x_der[:, q * E : (q + 1) * E] = stacked(value)
            for c in due:
                integ[c, q] = wt[5 * c : 5 * c + 1, :] * value

        @pl.loop(0, 4)
        def _(j):
            moved[0:E, :] = dot(a_ck[...], x_der[...])

            @pl.loop(0, 3)
            def _(group):
                acc = [None, None, None]
                for d in range(3):
                    acc = star_terms(acc, star, d, d * KP, group, -1)
                for pp in range(3):
                    p = group * 3 + pp
                    x_der[:, lanes(p)] = stacked(acc[pp])
                    for c in due:
                        integ[c, p] = integ[c, p] + wt[pl.ds(5 * c + 1 + j, 1), :] * acc[pp]

    def pack(c, route):
        for q in range(Q):
            comp[32 * q : 32 * q + 32, :] = integ[c, q, 0:32, :]
        for q in range(Q):
            comp[TAIL + 3 * q : TAIL + 3 * q + 8, :] = integ[c, q, 32:40, :]
        high, low = halves(comp[...])
        comp_h[c] = jnp.concatenate([high, low], axis=1).astype(BF16)
        picks = pick_send[c]
        packed[...] = dot(comp_h[c], jnp.concatenate([picks, picks], axis=0))

        @pl.loop(0, REACH)
        def _(r):
            for chunk in range(PIECE // 16):
                parts = [
                    packed[PIECE * g + 16 * chunk : PIECE * g + 16 * chunk + 16, lanes(r)]
                    for g in range(4)
                ]
                for t, part in enumerate(exchanged(parts, low_half, even)):
                    send[route, r * N_SUB + t, 16 * chunk : 16 * chunk + 16, :] = part

        recv[route, 2 * N_SUB + sub] = send[route, 2 * N_SUB + sub]

    def ghost_copy(route, out_idx, landing, peer, t):
        return pltpu.make_async_remote_copy(
            src_ref=send.at[route, out_idx],
            dst_ref=recv.at[route, landing],
            send_sem=send_sem.at[route, out_idx],
            recv_sem=recv_sem.at[route, landing],
            device_id=(peer, t),
            device_id_type=MESH,
        )

    def send_route(route):
        @pl.loop(0, PEERS)
        def _(idx):
            peer, t, valid = out_peer(idx)

            @pl.when(valid)
            def _():
                ghost_copy(route, idx, (idx // N_SUB) * N_SUB + sub, peer, t).start()

    def local_gather(c, first):
        picks = pick[c, 0]
        value = dot(comp_h[c], jnp.concatenate([picks, picks], axis=0))
        if first:
            got[...] = value
        else:
            got[...] += value

    def ghost_gather(c, route):
        @pl.loop(0, REACH)
        def _(r):
            for t in range(N_SUB):
                idx = r * N_SUB + t
                peer, _, valid = in_peer(idx)

                @pl.when(valid)
                def _():
                    ghost_copy(route, idx, idx, peer, t).wait_recv()

            for chunk in range(PIECE // 16):
                parts = [
                    recv[route, r * N_SUB + t, 16 * chunk : 16 * chunk + 16, :]
                    for t in range(N_SUB)
                ]
                for g, part in enumerate(exchanged(parts, low_half, even)):
                    start = PIECE * g + 16 * chunk
                    high, low = halves(part)
                    ghost[start : start + 16, 0:E] = high.astype(BF16)
                    ghost[start : start + 16, E : 2 * E] = low.astype(BF16)
            picks = pick[c, 1 + r]
            got[...] += dot(ghost[...], jnp.concatenate([picks, picks], axis=0))

    def own_columns(due):
        for q in range(Q):
            own = None
            for c in due:
                part = jnp.where(cluster_of == c, integ[c, q], 0.0)
                own = part if own is None else own + part
            x_own[:, q * E : (q + 1) * E] = stacked(own)

    def far_copy(s):
        return pltpu.make_async_remote_copy(
            src_ref=fsend.at[s],
            dst_ref=frecv.at[s],
            send_sem=fsend_sem.at[s],
            recv_sem=frecv_sem.at[s],
            device_id=(dom, (sub + 2) % N_SUB),
            device_id_type=MESH,
        )

    def send_near(s):
        moved[0:64, :] = dot(a_tr[...], x_own[...])
        marks = [cfe[16:17, :] == (i + 1.0) for i in range(4)]
        for q in range(Q):
            value = jnp.zeros((16, E), F32)
            for i in range(4):
                part = moved[16 * i : 16 * i + 16, q * E : (q + 1) * E]
                value = value + jnp.where(marks[i], part, 0.0)
            near[16 * q : 16 * q + 16, :] = value
        folded = None
        for g in range(4):
            high, low = halves(near[KP * g : KP * g + KP, :])
            part = dot(jnp.concatenate([high, low], axis=0).astype(BF16), pick_f[g])
            part = part[0:KP] + part[KP : 2 * KP]
            folded = part if folded is None else folded + part
        fsend[s] = folded
        far_copy(s).start()

    def volume():
        moved[...] = dot(a_vol[...], x_own[...])

        @pl.loop(0, 3)
        def _(group):
            acc = [cur[group * 3 + pp] for pp in range(3)]
            for d in range(3):
                acc = star_terms(acc, star, d, d * KP, group, 1)
            for i in range(4):
                acc = star_terms(acc, lsol, i, (3 + i) * KP, group, -1)
            for pp in range(3):
                cur[group * 3 + pp] = acc[pp]

    def fault(s):
        far_copy(s).wait_recv()
        high, low = halves(frecv[s])
        value = jnp.concatenate([high, low], axis=0).astype(BF16)
        for g in range(4):
            part = dot(value, pick_ft[g])
            far[KP * g : KP * g + KP, :] = part[0:KP] + part[KP : 2 * KP]
        for q in range(Q):
            mine, other = near[16 * q : 16 * q + 16, :], far[16 * q : 16 * q + 16, :]
            state = 0.5 * (mine + other) + cfe[q : q + 1, :] * (other - mine)
            high, low = halves(state)
            cols = slice(q * E, (q + 1) * E)
            x_state[0:48, cols] = jnp.concatenate([high, low, high], axis=0).astype(BF16)
        lift[...] = dot(a_li[...], x_state[...])

    def neighbours():
        @pl.loop(0, 4)
        def _(i):
            for q in range(Q):
                main = got[32 * q : 32 * q + 32, lanes(i)]
                tail = got[TAIL + 3 * q : TAIL + 3 * q + 8, lanes(i)]
                x_nbr[:, q * E : (q + 1) * E] = stacked(jnp.concatenate([main, tail], axis=0))
            across[...] = dot(a_nf[i], x_nbr[...])
            which = nface[pl.ds(i, 1), :]
            mark = cfe[16:17, :] == (i + 1).astype(F32)
            at = pl.multiple_of(i * KP, 8)
            for q in range(Q):
                cols = slice(q * E, (q + 1) * E)
                value = across[3 * KP : 4 * KP, cols]
                for j in range(2, -1, -1):
                    value = jnp.where(which == j, across[j * KP : (j + 1) * KP, cols], value)
                lifted[pl.ds(at, KP), cols] = value + jnp.where(mark, lift[pl.ds(at, KP), cols], 0.0)

        @pl.loop(0, 3)
        def _(group):
            acc = [cur[group * 3 + pp] for pp in range(3)]
            for i in range(4):
                for q in range(Q):
                    value = lifted[i * KP : (i + 1) * KP, q * E : (q + 1) * E]
                    for pp in range(3):
                        acc[pp] = acc[pp] - nsol[i, group * 3 + pp, q : q + 1, :] * value
            for pp in range(3):
                cur[group * 3 + pp] = acc[pp]

    def prepare_pick_send(c):
        for r in range(REACH):
            row = tab[c, r : r + 1, :]
            pick_send[c, :, r * E : (r + 1) * E] = jnp.where(element_rows == row, 1.0, 0.0).astype(BF16)

    def prepare_pick(c):
        @pl.loop(0, 1 + REACH)
        def _(g):
            for i in range(4):
                row = jnp.where(cluster_of == c, fnbr[i : i + 1, :] - E * g, -1)
                cols = slice(i * E, (i + 1) * E)
                pick[c, g, :, cols] = jnp.where(element_rows == row, 1.0, 0.0).astype(BF16)

    derive(0, (0, 1, 2))
    for c in range(3):
        for r in range(REACH):
            for t in range(N_SUB):
                tab[c, r : r + 1, SLOT * t : SLOT * (t + 1)] = stab[c, r, t : t + 1, :]
    prepare_pick_send(0)
    pack(0, ROUTES[0, 0])

    @pl.loop(0, REACH)
    def _(r):
        peer = dom - r + 2

        @pl.when((peer < 0) | (peer >= n_dom))
        def _():
            @pl.loop(0, len(ROUTES))
            def _(route):
                for t in range(N_SUB):
                    recv[route, r * N_SUB + t] = jnp.zeros((PIECE, E), F32)

    groups = jnp.minimum(dom + 2, n_dom - 1) - jnp.maximum(dom - 2, 0) + 1
    pl.semaphore_wait(barrier, groups * N_SUB - 1)
    send_route(ROUTES[0, 0])

    own_columns((0, 1, 2))
    wide_at = 3
    for i in range(4):
        wide[wide_at + i, :FB, :B] = ftrace[i]
    a_tr[...] = jnp.concatenate(
        [weights(wide[wide_at + i, 0:16, :], KP) for i in range(4)], axis=0
    ).astype(BF16)
    wide_at += 4
    fer[...] = jnp.full(fer.shape, -1, jnp.int32)
    for g in range(4):
        fer[g : g + 1, NF * g : NF * (g + 1)] = felem[...]
    for g in range(4):
        spot = jnp.where(element_rows == fer[g : g + 1, :], 1.0, 0.0)
        pick_f[g] = spot.astype(BF16)
        pick_ft[g] = spot.T.astype(BF16)
    cfs[...] = jnp.zeros(cfs.shape, F32)
    cfs[0:Q, 0:NF] = fcoef[...]
    cfs[16:17, 0:NF] = (fface[...] + 1).astype(F32)
    high, low = halves(cfs[...])
    spread = dot(jnp.concatenate([high, low], axis=0).astype(BF16), pick_ft[0])
    cfe[...] = spread[0:32] + spread[32:64]
    near[...] = jnp.zeros(near.shape, F32)
    x_state[...] = jnp.zeros(x_state.shape, BF16)
    send_near(0)

    for c in (1, 2):
        prepare_pick_send(c)
        pack(c, ROUTES[0, c])

    for d in range(3):
        wide[wide_at + d, :B, :B] = stiff[d]
    for i in range(4):
        wide[wide_at + 3 + i, :B, :B] = lflux[i]
    a_vol[...] = jnp.concatenate(
        [weights(wide[wide_at + m], KP) for m in range(7)] + [jnp.zeros((8, E), F32)], axis=0
    ).astype(BF16)
    wide_at += 7
    volume()
    prepare_pick(0)
    for i in range(4):
        for j in range(4):
            wide[wide_at + 4 * i + j, :B, :B] = nflux[i, j]
        a_nf[i] = jnp.concatenate(
            [weights(wide[wide_at + 4 * i + j], KP) for j in range(4)], axis=0
        ).astype(BF16)
    wide_at += 16
    for i in range(4):
        wide[wide_at + i, :B, :FB] = flift[i]
    a_li[...] = jnp.concatenate(
        [weights(wide[wide_at + i], 16) for i in range(4)], axis=0
    ).astype(BF16)
    local_gather(0, True)
    fault(0)
    prepare_pick(1)
    ghost_gather(0, ROUTES[0, 0])
    send_route(ROUTES[0, 1])
    neighbours()

    local_gather(1, True)
    derive(1, (0,))
    pack(0, ROUTES[1, 0])
    send_route(ROUTES[1, 0])
    own_columns((0,))
    send_near(1)
    volume()
    local_gather(0, False)
    prepare_pick(2)
    ghost_gather(1, ROUTES[0, 1])
    fault(1)
    ghost_gather(0, ROUTES[1, 0])
    send_route(ROUTES[0, 2])
    neighbours()

    local_gather(2, True)
    derive(2, (0, 1))
    pack(0, ROUTES[2, 0])
    send_route(ROUTES[2, 0])
    own_columns((0, 1))
    send_near(2)
    pack(1, ROUTES[2, 1])
    volume()
    local_gather(0, False)
    ghost_gather(2, ROUTES[0, 2])
    fault(2)
    ghost_gather(0, ROUTES[2, 0])
    send_route(ROUTES[2, 1])
    neighbours()

    local_gather(1, True)
    derive(3, (0,))
    pack(0, ROUTES[3, 0])
    send_route(ROUTES[3, 0])
    own_columns((0,))
    send_near(3)
    volume()
    local_gather(0, False)
    ghost_gather(1, ROUTES[2, 1])
    fault(3)
    ghost_gather(0, ROUTES[3, 0])
    neighbours()
    out[...] = cur[:, :B, :]

    @pl.loop(0, len(ROUTES))
    def _(route):
        @pl.loop(0, PEERS)
        def _(idx):
            peer, t, valid = out_peer(idx)

            @pl.when(valid)
            def _():
                ghost_copy(route, idx, (idx // N_SUB) * N_SUB + sub, peer, t).wait_send()

    for s in range(4):
        far_copy(s).wait_send()


def body(n_dom, *args):
    args = list(args)
    for index in (4, 8, 9):
        args[index] = args[index].reshape(1, -1)
    routes = len(ROUTES)
    scratch = [
        pltpu.VMEM((Q, KP, E), F32),
        pltpu.VMEM((Q, KP, E), F32),
        pltpu.VMEM((3, Q, KP, E), F32),
        pltpu.VMEM((E, W), BF16),
        pltpu.VMEM((E, W), BF16),
        pltpu.VMEM((E, W), BF16),
        pltpu.VMEM((E, W), BF16),
        pltpu.VMEM((288, W), F32),
        pltpu.VMEM((4 * KP, W), F32),
        pltpu.VMEM((4 * KP, W), F32),
        pltpu.VMEM((4 * KP, W), F32),
        pltpu.VMEM((4 * KP, E), F32),
        pltpu.VMEM((4 * KP, E), F32),
        pltpu.VMEM((4, KP, E), F32),
        pltpu.VMEM((4, KP, E), F32),
        pltpu.VMEM((ROWS, E), F32),
        pltpu.VMEM((3, ROWS, 2 * E), BF16),
        pltpu.VMEM((ROWS, 4 * E), F32),
        pltpu.VMEM((ROWS, 2 * E), BF16),
        pltpu.VMEM((ROWS, REACH * E), F32),
        pltpu.VMEM((3, 1 + REACH, E, 4 * E), BF16),
        pltpu.VMEM((3, E, REACH * E), BF16),
        pltpu.VMEM((4, E, E), BF16),
        pltpu.VMEM((4, E, E), BF16),
        pltpu.VMEM((E, E), BF16),
        pltpu.VMEM((288, E), BF16),
        pltpu.VMEM((4, 4 * KP, E), BF16),
        pltpu.VMEM((64, E), BF16),
        pltpu.VMEM((4 * KP, E), BF16),
        pltpu.VMEM((34, KP, E), F32),
        pltpu.VMEM((3, 8, E), jnp.int32),
        pltpu.VMEM((8, E), jnp.int32),
        pltpu.VMEM((32, E), F32),
        pltpu.VMEM((32, E), F32),
        pltpu.VMEM((16, E), F32),
        pltpu.VMEM((routes, PEERS, PIECE, E), F32),
        pltpu.VMEM((routes, PEERS, PIECE, E), F32),
        pltpu.SemaphoreType.DMA((routes, PEERS)),
        pltpu.SemaphoreType.DMA((routes, PEERS)),
        pltpu.SemaphoreType.DMA((4,)),
        pltpu.SemaphoreType.DMA((4,)),
    ]
    return pl.pallas_call(
        functools.partial(kernel, n_dom),
        out_shape=jax.ShapeDtypeStruct((Q, B, E), F32),
        in_specs=[pl.BlockSpec(memory_space=pltpu.VMEM)] * len(args),
        out_specs=pl.BlockSpec(memory_space=pltpu.VMEM),
        scratch_shapes=scratch,
        compiler_params=pltpu.CompilerParams(
            collective_id=0, has_side_effects=True, vmem_limit_bytes=48 * 1024 * 1024
        ),
    )(*args)


def solution(mesh):
    in_specs = (
        P(None, None, ("dom", "sub")),
        P(None, None, None, ("dom", "sub")),
        P(None, None, None, ("dom", "sub")),
        P(None, None, None, ("dom", "sub")),
        P(("dom", "sub")),
        P(None, ("dom", "sub")),
        P(None, ("dom", "sub")),
        P(("dom", "sub"), None, None, None),
        P(("dom", "sub")),
        P(("dom", "sub")),
        P(None, ("dom", "sub")),
        P(),
        P(),
        P(),
        P(),
        P(),
        P(),
    )
    out_specs = P(None, None, ("dom", "sub"))
    return jax.shard_map(
        functools.partial(body, mesh.shape["dom"]),
        mesh=mesh,
        in_specs=in_specs,
        out_specs=out_specs,
        check_vma=False,
    )
```

```python
import functools

import jax
import jax.numpy as jnp
from jax import lax
from jax.experimental import pallas as pl
from jax.experimental.pallas import tpu as pltpu
from jax.sharding import PartitionSpec as P

MESH = pl.DeviceIdType.MESH
F32 = jnp.float32
BF16 = jnp.bfloat16
Q = 9
B = 35
KP = 40
E = 128
W = Q * E
FB = 15
NF = 32
SLOT = 32
REACH = 5
N_SUB = 4
PEERS = REACH * N_SUB
ROWS = 320
PIECE = ROWS // N_SUB
TAIL = Q * 32
STEP = 0.25
ROUTES = {(0, 0): 0, (0, 1): 1, (0, 2): 2, (1, 0): 3, (2, 0): 4, (2, 1): 5, (3, 0): 6}


def halves(value):
    high = value.astype(BF16).astype(F32)
    return high, value - high


def stacked(value):
    high, low = halves(value)
    return jnp.concatenate([high, low, high, jnp.zeros((8, E), F32)], axis=0).astype(BF16)


def weights(matrix, width):
    high, low = halves(matrix)
    return high + pltpu.roll(high, width, 1) + pltpu.roll(low, 2 * width, 1)


def dot(left, right):
    return jnp.dot(left, right, preferred_element_type=F32)


def lanes(index, count=1):
    return pl.ds(pl.multiple_of(index * E, E), count * E)


def exchanged(parts, low_half, even):
    mixed = [None] * 4
    for g in range(2):
        mixed[g] = jnp.where(low_half, parts[g], pltpu.roll(parts[g + 2], 64, 1))
        mixed[g + 2] = jnp.where(low_half, pltpu.roll(parts[g], 64, 1), parts[g + 2])
    out = [None] * 4
    for g in (0, 2):
        out[g] = jnp.where(even, mixed[g], pltpu.roll(mixed[g + 1], 32, 1))
        out[g + 1] = jnp.where(even, pltpu.roll(mixed[g], 96, 1), mixed[g + 1])
    return out


def kernel(
    n_dom,
    dofs_hbm,
    star_hbm,
    lsol_hbm,
    nsol_hbm,
    ecl_hbm,
    fnbr_hbm,
    nface_hbm,
    stab_hbm,
    felem_hbm,
    fface_hbm,
    fcoef_hbm,
    ck_hbm,
    stiff_hbm,
    lflux_hbm,
    nflux_hbm,
    ftrace_hbm,
    flift_hbm,
    out,
    dofs,
    star,
    lsol,
    nsol,
    ecl,
    fnbr,
    nface,
    stab,
    felem,
    fface,
    fcoef,
    ck,
    stiff,
    lflux,
    nflux,
    ftrace,
    flift,
    base,
    cur,
    integ,
    x_der,
    x_own,
    x_nbr,
    x_state,
    moved,
    across,
    lifted,
    lift,
    near,
    far,
    fsend,
    frecv,
    comp,
    comp_h,
    got,
    ghost,
    packed,
    pick,
    pick_send,
    pick_f,
    pick_ft,
    a_ck,
    a_vol,
    a_nf,
    a_tr,
    a_li,
    wide,
    sides_in,
    tab,
    fer,
    cfs,
    cfe,
    wt,
    send,
    recv,
    send_sem,
    recv_sem,
    fsend_sem,
    frecv_sem,
    load_sem,
):
    dom = lax.axis_index("dom")
    sub = lax.axis_index("sub")

    def out_peer(idx):
        r, t = idx // N_SUB, idx % N_SUB
        peer = dom + r - 2
        valid = (peer >= 0) & (peer < n_dom) & jnp.logical_not((r == 2) & (t == sub))
        return peer, t, valid

    def in_peer(idx):
        r, t = idx // N_SUB, idx % N_SUB
        peer = dom - r + 2
        valid = (peer >= 0) & (peer < n_dom) & jnp.logical_not((r == 2) & (t == sub))
        return peer, t, valid

    loads = [
        pltpu.make_async_copy(source, target, load_sem.at[k])
        for k, (source, target) in enumerate(
            (
                (dofs_hbm, dofs),
                (ck_hbm, ck),
                (ecl_hbm, ecl),
                (star_hbm, star),
                (stab_hbm, stab),
                (felem_hbm, felem),
                (fface_hbm, fface),
                (fcoef_hbm, fcoef),
                (ftrace_hbm, ftrace),
                (stiff_hbm, stiff),
                (lflux_hbm, lflux),
                (lsol_hbm, lsol),
                (fnbr_hbm, fnbr),
                (nface_hbm, nface),
                (flift_hbm, flift),
                (nflux_hbm, nflux),
                (nsol_hbm, nsol),
            )
        )
    ]
    for load in loads:
        load.start()
    barrier = pltpu.get_barrier_semaphore()

    @pl.loop(0, PEERS)
    def _(idx):
        peer, t, valid = out_peer(idx)

        @pl.when(valid)
        def _():
            pl.semaphore_signal(barrier, inc=1, device_id=(peer, t), device_id_type=MESH)

    lane = lax.broadcasted_iota(jnp.int32, (16, E), 1)
    low_half = lane < 64
    even = (lane // 32) % 2 == 0
    element_rows = lax.broadcasted_iota(jnp.int32, (E, E), 0)

    for load in loads[:5]:
        load.wait()
    base[...] = jnp.zeros((Q, KP, E), F32)
    base[:, :B, :] = dofs[...]
    cur[...] = base[...]
    wide[...] = jnp.zeros(wide.shape, F32)
    for d in range(3):
        wide[d, :B, :B] = ck[d]
    a_ck[...] = jnp.concatenate(
        [weights(wide[d], KP) for d in range(3)] + [jnp.zeros((8, E), F32)], axis=0
    ).astype(BF16)
    cluster_of = ecl[...]

    def star_terms(acc, coef, first, rows, group, sign):
        for q in range(Q):
            value = moved[rows : rows + KP, q * E : (q + 1) * E]
            for pp in range(3):
                term = coef[group * 3 + pp, q, first : first + 1, :] * value
                if acc[pp] is None:
                    acc[pp] = term if sign > 0 else -term
                else:
                    acc[pp] = acc[pp] + term if sign > 0 else acc[pp] - term
        return acc

    def derive(s, due):
        if s > 0:
            keep = cluster_of == 0
            if s % 2 == 0:
                keep = cluster_of <= 1
            for q in range(Q):
                base[q] = jnp.where(keep, cur[q], base[q])
        offset = jnp.where(
            cluster_of == 0, 0.0, jnp.where(cluster_of == 1, (s % 2) * STEP, (s % 4) * STEP)
        ).astype(F32)
        for c in due:
            end = offset + STEP * 2**c
            upper, lower, factor = end, offset, 1.0
            for j in range(5):
                factor = factor * (j + 1)
                wt[5 * c + j : 5 * c + j + 1, :] = (upper - lower) * (1.0 / factor)
                upper, lower = upper * end, lower * offset
        for q in range(Q):
            value = base[q]
            x_der[:, q * E : (q + 1) * E] = stacked(value)
            for c in due:
                integ[c, q] = wt[5 * c : 5 * c + 1, :] * value

        @pl.loop(0, 4)
        def _(j):
            moved[0:E, :] = dot(a_ck[...], x_der[...])

            @pl.loop(0, 3)
            def _(group):
                acc = [None, None, None]
                for d in range(3):
                    acc = star_terms(acc, star, d, d * KP, group, -1)
                for pp in range(3):
                    p = group * 3 + pp
                    x_der[:, lanes(p)] = stacked(acc[pp])
                    for c in due:
                        integ[c, p] = integ[c, p] + wt[pl.ds(5 * c + 1 + j, 1), :] * acc[pp]

    def pack(c, route, now=False):
        for q in range(Q):
            comp[32 * q : 32 * q + 32, :] = integ[c, q, 0:32, :]
        for q in range(Q):
            comp[TAIL + 3 * q : TAIL + 3 * q + 8, :] = integ[c, q, 32:40, :]
        high, low = halves(comp[...])
        comp_h[c] = jnp.concatenate([high, low], axis=1).astype(BF16)
        picks = pick_send[c]
        packed[...] = dot(comp_h[c], jnp.concatenate([picks, picks], axis=0))

        @pl.loop(0, REACH)
        def _(r):
            for chunk in range(PIECE // 16):
                parts = [
                    packed[PIECE * g + 16 * chunk : PIECE * g + 16 * chunk + 16, lanes(r)]
                    for g in range(4)
                ]
                for t, part in enumerate(exchanged(parts, low_half, even)):
                    send[route, r * N_SUB + t, 16 * chunk : 16 * chunk + 16, :] = part
            if now:
                send_block(route, r)

        recv[route, 2 * N_SUB + sub] = send[route, 2 * N_SUB + sub]

    def ghost_copy(route, out_idx, landing, peer, t):
        return pltpu.make_async_remote_copy(
            src_ref=send.at[route, out_idx],
            dst_ref=recv.at[route, landing],
            send_sem=send_sem.at[route, out_idx],
            recv_sem=recv_sem.at[route, landing],
            device_id=(peer, t),
            device_id_type=MESH,
        )

    def send_block(route, r):
        for t in range(N_SUB):
            idx = r * N_SUB + t
            peer, _, valid = out_peer(idx)

            @pl.when(valid)
            def _():
                ghost_copy(route, idx, r * N_SUB + sub, peer, t).start()

    def local_gather(c, first):
        picks = pick[c, 0]
        value = dot(comp_h[c], jnp.concatenate([picks, picks], axis=0))
        if first:
            got[...] = value
        else:
            got[...] += value

    def ghost_gather(c, route, then=None):
        if then is not None:
            for r in range(1):
                send_block(then, r)
        @pl.loop(0, REACH)
        def _(r):
            for t in range(N_SUB):
                idx = r * N_SUB + t
                peer, _, valid = in_peer(idx)

                @pl.when(valid)
                def _():
                    ghost_copy(route, idx, idx, peer, t).wait_recv()

            if then is not None:

                @pl.when(r + 1 < REACH)
                def _():
                    send_block(then, r + 1)

            for chunk in range(PIECE // 16):
                parts = [
                    recv[route, r * N_SUB + t, 16 * chunk : 16 * chunk + 16, :]
                    for t in range(N_SUB)
                ]
                for g, part in enumerate(exchanged(parts, low_half, even)):
                    start = PIECE * g + 16 * chunk
                    high, low = halves(part)
                    ghost[start : start + 16, 0:E] = high.astype(BF16)
                    ghost[start : start + 16, E : 2 * E] = low.astype(BF16)
            picks = pick[c, 1 + r]
            got[...] += dot(ghost[...], jnp.concatenate([picks, picks], axis=0))

    def own_columns(due):
        for q in range(Q):
            own = None
            for c in due:
                part = jnp.where(cluster_of == c, integ[c, q], 0.0)
                own = part if own is None else own + part
            x_own[:, q * E : (q + 1) * E] = stacked(own)

    def far_copy(s):
        return pltpu.make_async_remote_copy(
            src_ref=fsend.at[s],
            dst_ref=frecv.at[s],
            send_sem=fsend_sem.at[s],
            recv_sem=frecv_sem.at[s],
            device_id=(dom, (sub + 2) % N_SUB),
            device_id_type=MESH,
        )

    def send_near(s):
        moved[0:64, :] = dot(a_tr[...], x_own[...])
        marks = [cfe[16:17, :] == (i + 1.0) for i in range(4)]
        for q in range(Q):
            value = jnp.zeros((16, E), F32)
            for i in range(4):
                part = moved[16 * i : 16 * i + 16, q * E : (q + 1) * E]
                value = value + jnp.where(marks[i], part, 0.0)
            near[16 * q : 16 * q + 16, :] = value
        folded = None
        for g in range(4):
            high, low = halves(near[KP * g : KP * g + KP, :])
            part = dot(jnp.concatenate([high, low], axis=0).astype(BF16), pick_f[g])
            part = part[0:KP] + part[KP : 2 * KP]
            folded = part if folded is None else folded + part
        fsend[s] = folded
        far_copy(s).start()

    def volume():
        moved[...] = dot(a_vol[...], x_own[...])

        @pl.loop(0, 3)
        def _(group):
            acc = [cur[group * 3 + pp] for pp in range(3)]
            for d in range(3):
                acc = star_terms(acc, star, d, d * KP, group, 1)
            for i in range(4):
                acc = star_terms(acc, lsol, i, (3 + i) * KP, group, -1)
            for pp in range(3):
                cur[group * 3 + pp] = acc[pp]

    def fault(s):
        far_copy(s).wait_recv()
        high, low = halves(frecv[s])
        value = jnp.concatenate([high, low], axis=0).astype(BF16)
        for g in range(4):
            part = dot(value, pick_ft[g])
            far[KP * g : KP * g + KP, :] = part[0:KP] + part[KP : 2 * KP]
        for q in range(Q):
            mine, other = near[16 * q : 16 * q + 16, :], far[16 * q : 16 * q + 16, :]
            state = 0.5 * (mine + other) + cfe[q : q + 1, :] * (other - mine)
            high, low = halves(state)
            cols = slice(q * E, (q + 1) * E)
            x_state[0:48, cols] = jnp.concatenate([high, low, high], axis=0).astype(BF16)
        lift[...] = dot(a_li[...], x_state[...])

    def neighbours():
        @pl.loop(0, 4)
        def _(i):
            for q in range(Q):
                main = got[32 * q : 32 * q + 32, lanes(i)]
                tail = got[TAIL + 3 * q : TAIL + 3 * q + 8, lanes(i)]
                x_nbr[:, q * E : (q + 1) * E] = stacked(jnp.concatenate([main, tail], axis=0))
            across[...] = dot(a_nf[i], x_nbr[...])
            which = nface[pl.ds(i, 1), :]
            mark = cfe[16:17, :] == (i + 1).astype(F32)
            at = pl.multiple_of(i * KP, 8)
            for q in range(Q):
                cols = slice(q * E, (q + 1) * E)
                value = across[3 * KP : 4 * KP, cols]
                for j in range(2, -1, -1):
                    value = jnp.where(which == j, across[j * KP : (j + 1) * KP, cols], value)
                lifted[pl.ds(at, KP), cols] = value + jnp.where(mark, lift[pl.ds(at, KP), cols], 0.0)

        @pl.loop(0, 3)
        def _(group):
            acc = [cur[group * 3 + pp] for pp in range(3)]
            for i in range(4):
                for q in range(Q):
                    value = lifted[i * KP : (i + 1) * KP, q * E : (q + 1) * E]
                    for pp in range(3):
                        acc[pp] = acc[pp] - nsol[group * 3 + pp, q, i : i + 1, :] * value
            for pp in range(3):
                cur[group * 3 + pp] = acc[pp]

    def prepare_pick_send(c):
        for r in range(REACH):
            row = tab[c, r : r + 1, :]
            pick_send[c, :, r * E : (r + 1) * E] = jnp.where(element_rows == row, 1.0, 0.0).astype(BF16)

    def prepare_pick(c):
        @pl.loop(0, 1 + REACH)
        def _(g):
            for i in range(4):
                row = jnp.where(cluster_of == c, fnbr[i : i + 1, :] - E * g, -1)
                cols = slice(i * E, (i + 1) * E)
                pick[c, g, :, cols] = jnp.where(element_rows == row, 1.0, 0.0).astype(BF16)

    derive(0, (0, 1, 2))
    for c in range(3):
        for r in range(REACH):
            for t in range(N_SUB):
                tab[c, r : r + 1, SLOT * t : SLOT * (t + 1)] = stab[c, r, t : t + 1, :]
    prepare_pick_send(0)
    @pl.loop(0, REACH)
    def _(r):
        peer = dom - r + 2

        @pl.when((peer < 0) | (peer >= n_dom))
        def _():
            @pl.loop(0, len(ROUTES))
            def _(route):
                for t in range(N_SUB):
                    recv[route, r * N_SUB + t] = jnp.zeros((PIECE, E), F32)

    groups = jnp.minimum(dom + 2, n_dom - 1) - jnp.maximum(dom - 2, 0) + 1
    pl.semaphore_wait(barrier, groups * N_SUB - 1)

    pack(0, ROUTES[0, 0], True)


    for load in loads[5:9]:
        load.wait()
    own_columns((0, 1, 2))
    wide_at = 3
    for i in range(4):
        wide[wide_at + i, :FB, :B] = ftrace[:, i, :]
    a_tr[...] = jnp.concatenate(
        [weights(wide[wide_at + i, 0:16, :], KP) for i in range(4)], axis=0
    ).astype(BF16)
    wide_at += 4
    fer[...] = jnp.full(fer.shape, -1, jnp.int32)
    for g in range(4):
        fer[g : g + 1, NF * g : NF * (g + 1)] = felem[...]
    for g in range(4):
        spot = jnp.where(element_rows == fer[g : g + 1, :], 1.0, 0.0)
        pick_f[g] = spot.astype(BF16)
        pick_ft[g] = spot.T.astype(BF16)
    cfs[...] = jnp.zeros(cfs.shape, F32)
    cfs[0:Q, 0:NF] = fcoef[...]
    cfs[16:17, 0:NF] = (fface[...] + 1).astype(F32)
    high, low = halves(cfs[...])
    spread = dot(jnp.concatenate([high, low], axis=0).astype(BF16), pick_ft[0])
    cfe[...] = spread[0:32] + spread[32:64]
    near[...] = jnp.zeros(near.shape, F32)
    x_state[...] = jnp.zeros(x_state.shape, BF16)
    send_near(0)

    for c in (1, 2):
        prepare_pick_send(c)
        pack(c, ROUTES[0, c])

    for load in loads[9:]:
        load.wait()
    for d in range(3):
        wide[wide_at + d, :B, :B] = stiff[d]
    for i in range(4):
        wide[wide_at + 3 + i, :B, :B] = lflux[:, i, :]
    a_vol[...] = jnp.concatenate(
        [weights(wide[wide_at + m], KP) for m in range(7)] + [jnp.zeros((8, E), F32)], axis=0
    ).astype(BF16)
    wide_at += 7
    volume()
    prepare_pick(0)
    for i in range(4):
        for j in range(4):
            wide[wide_at + 4 * i + j, :B, :B] = nflux[i, :, j, :]
        a_nf[i] = jnp.concatenate(
            [weights(wide[wide_at + 4 * i + j], KP) for j in range(4)], axis=0
        ).astype(BF16)
    wide_at += 16
    sides_in[...] = jnp.zeros((E, E), F32)
    for i in range(4):
        sides_in[16 * i : 16 * i + FB, :B] = flift[:, i, :]
    sides = sides_in[...].T[0:KP]
    first = lax.broadcasted_iota(jnp.int32, (KP, E), 1) < 16
    parts = [jnp.where(first, pltpu.roll(sides, (E - 16 * i) % E, 1), 0.0) for i in range(4)]
    a_li[...] = jnp.concatenate([weights(part, 16) for part in parts], axis=0).astype(BF16)
    local_gather(0, True)
    fault(0)
    prepare_pick(1)
    ghost_gather(0, ROUTES[0, 0], ROUTES[0, 1])
    neighbours()

    local_gather(1, True)
    derive(1, (0,))
    pack(0, ROUTES[1, 0], True)
    own_columns((0,))
    send_near(1)
    volume()
    local_gather(0, False)
    prepare_pick(2)
    ghost_gather(1, ROUTES[0, 1])
    fault(1)
    ghost_gather(0, ROUTES[1, 0], ROUTES[0, 2])
    neighbours()

    local_gather(2, True)
    derive(2, (0, 1))
    pack(0, ROUTES[2, 0], True)
    own_columns((0, 1))
    send_near(2)
    pack(1, ROUTES[2, 1])
    volume()
    local_gather(0, False)
    ghost_gather(2, ROUTES[0, 2])
    fault(2)
    ghost_gather(0, ROUTES[2, 0], ROUTES[2, 1])
    neighbours()

    local_gather(1, True)
    derive(3, (0,))
    pack(0, ROUTES[3, 0], True)
    own_columns((0,))
    send_near(3)
    volume()
    local_gather(0, False)
    ghost_gather(1, ROUTES[2, 1])
    fault(3)
    ghost_gather(0, ROUTES[3, 0])
    neighbours()
    out[...] = cur[:, :B, :]

    @pl.loop(0, len(ROUTES))
    def _(route):
        @pl.loop(0, PEERS)
        def _(idx):
            peer, t, valid = out_peer(idx)

            @pl.when(valid)
            def _():
                ghost_copy(route, idx, (idx // N_SUB) * N_SUB + sub, peer, t).wait_send()

    for s in range(4):
        far_copy(s).wait_send()


def body(n_dom, *args):
    args = list(args)
    for index in (4, 8, 9):
        args[index] = args[index].reshape(1, -1)
    for index, order in ((1, (1, 2, 0, 3)), (2, (1, 2, 0, 3)), (3, (1, 2, 0, 3))):
        args[index] = args[index].transpose(order)
    for index, order in ((13, (1, 0, 2)), (14, (0, 2, 1, 3)), (15, (1, 0, 2)), (16, (2, 0, 1))):
        args[index] = args[index].transpose(order)
    specs = [pl.BlockSpec(memory_space=pltpu.HBM)] * len(args)
    routes = len(ROUTES)
    scratch = [pltpu.VMEM(arg.shape, arg.dtype) for arg in args] + [
        pltpu.VMEM((Q, KP, E), F32),
        pltpu.VMEM((Q, KP, E), F32),
        pltpu.VMEM((3, Q, KP, E), F32),
        pltpu.VMEM((E, W), BF16),
        pltpu.VMEM((E, W), BF16),
        pltpu.VMEM((E, W), BF16),
        pltpu.VMEM((E, W), BF16),
        pltpu.VMEM((288, W), F32),
        pltpu.VMEM((4 * KP, W), F32),
        pltpu.VMEM((4 * KP, W), F32),
        pltpu.VMEM((4 * KP, W), F32),
        pltpu.VMEM((4 * KP, E), F32),
        pltpu.VMEM((4 * KP, E), F32),
        pltpu.VMEM((4, KP, E), F32),
        pltpu.VMEM((4, KP, E), F32),
        pltpu.VMEM((ROWS, E), F32),
        pltpu.VMEM((3, ROWS, 2 * E), BF16),
        pltpu.VMEM((ROWS, 4 * E), F32),
        pltpu.VMEM((ROWS, 2 * E), BF16),
        pltpu.VMEM((ROWS, REACH * E), F32),
        pltpu.VMEM((3, 1 + REACH, E, 4 * E), BF16),
        pltpu.VMEM((3, E, REACH * E), BF16),
        pltpu.VMEM((4, E, E), BF16),
        pltpu.VMEM((4, E, E), BF16),
        pltpu.VMEM((E, E), BF16),
        pltpu.VMEM((288, E), BF16),
        pltpu.VMEM((4, 4 * KP, E), BF16),
        pltpu.VMEM((64, E), BF16),
        pltpu.VMEM((4 * KP, E), BF16),
        pltpu.VMEM((30, KP, E), F32),
        pltpu.VMEM((E, E), F32),
        pltpu.VMEM((3, 8, E), jnp.int32),
        pltpu.VMEM((8, E), jnp.int32),
        pltpu.VMEM((32, E), F32),
        pltpu.VMEM((32, E), F32),
        pltpu.VMEM((16, E), F32),
        pltpu.VMEM((routes, PEERS, PIECE, E), F32),
        pltpu.VMEM((routes, PEERS, PIECE, E), F32),
        pltpu.SemaphoreType.DMA((routes, PEERS)),
        pltpu.SemaphoreType.DMA((routes, PEERS)),
        pltpu.SemaphoreType.DMA((4,)),
        pltpu.SemaphoreType.DMA((4,)),
        pltpu.SemaphoreType.DMA((17,)),
    ]
    return pl.pallas_call(
        functools.partial(kernel, n_dom),
        out_shape=jax.ShapeDtypeStruct((Q, B, E), F32),
        in_specs=specs,
        out_specs=pl.BlockSpec(memory_space=pltpu.VMEM),
        scratch_shapes=scratch,
        compiler_params=pltpu.CompilerParams(
            collective_id=0, has_side_effects=True, vmem_limit_bytes=60 * 1024 * 1024
        ),
    )(*args)


def solution(mesh):
    in_specs = (
        P(None, None, ("dom", "sub")),
        P(None, None, None, ("dom", "sub")),
        P(None, None, None, ("dom", "sub")),
        P(None, None, None, ("dom", "sub")),
        P(("dom", "sub")),
        P(None, ("dom", "sub")),
        P(None, ("dom", "sub")),
        P(("dom", "sub"), None, None, None),
        P(("dom", "sub")),
        P(("dom", "sub")),
        P(None, ("dom", "sub")),
        P(),
        P(),
        P(),
        P(),
        P(),
        P(),
    )
    out_specs = P(None, None, ("dom", "sub"))
    return jax.shard_map(
        functools.partial(body, mesh.shape["dom"]),
        mesh=mesh,
        in_specs=in_specs,
        out_specs=out_specs,
        check_vma=False,
    )
```

```python
import functools

import jax
import jax.numpy as jnp
from jax import lax
from jax.experimental import pallas as pl
from jax.experimental.pallas import tpu as pltpu
from jax.sharding import PartitionSpec as P

MESH = pl.DeviceIdType.MESH
F32 = jnp.float32
BF16 = jnp.bfloat16
Q = 9
B = 35
KP = 40
E = 128
W = Q * E
FB = 15
NF = 32
SLOT = 32
REACH = 5
N_SUB = 4
PEERS = REACH * N_SUB
ROWS = 320
PIECE = ROWS // N_SUB
TAIL = Q * 32
STEP = 0.25
ROUTES = {(0, 0): 0, (0, 1): 1, (0, 2): 2, (1, 0): 3, (2, 0): 4, (2, 1): 5, (3, 0): 6}


def halves(value):
    high = value.astype(BF16).astype(F32)
    return high, value - high


def stacked(value):
    high, low = halves(value)
    return jnp.concatenate([high, low, high, jnp.zeros((8, E), F32)], axis=0).astype(BF16)


def weights(matrix, width):
    high, low = halves(matrix)
    return high + pltpu.roll(high, width, 1) + pltpu.roll(low, 2 * width, 1)


def dot(left, right):
    return jnp.dot(left, right, preferred_element_type=F32)


def lanes(index, count=1):
    return pl.ds(pl.multiple_of(index * E, E), count * E)


def exchanged(parts, low_half, even):
    mixed = [None] * 4
    for g in range(2):
        mixed[g] = jnp.where(low_half, parts[g], pltpu.roll(parts[g + 2], 64, 1))
        mixed[g + 2] = jnp.where(low_half, pltpu.roll(parts[g], 64, 1), parts[g + 2])
    out = [None] * 4
    for g in (0, 2):
        out[g] = jnp.where(even, mixed[g], pltpu.roll(mixed[g + 1], 32, 1))
        out[g + 1] = jnp.where(even, pltpu.roll(mixed[g], 96, 1), mixed[g + 1])
    return out


def kernel(
    n_dom,
    dofs_hbm,
    star_hbm,
    lsol_hbm,
    nsol_hbm,
    ecl_hbm,
    fnbr_hbm,
    nface_hbm,
    stab_hbm,
    felem_hbm,
    fface_hbm,
    fcoef_hbm,
    ck_hbm,
    stiff_hbm,
    lflux_hbm,
    nflux_hbm,
    ftrace_hbm,
    flift_hbm,
    out,
    dofs,
    star,
    lsol,
    nsol,
    ecl,
    fnbr,
    nface,
    stab,
    felem,
    fface,
    fcoef,
    ck,
    stiff,
    lflux,
    nflux,
    ftrace,
    flift,
    base,
    cur,
    integ,
    x_der,
    x_own,
    x_nbr,
    x_state,
    moved,
    across,
    lifted,
    lift,
    near,
    far,
    fsend,
    frecv,
    comp,
    comp_h,
    got,
    ghost,
    packed,
    pick,
    pick_send,
    pick_f,
    pick_ft,
    a_ck,
    a_vol,
    a_nf,
    a_tr,
    a_li,
    wide,
    sides_in,
    tab,
    fer,
    cfs,
    cfe,
    wt,
    send,
    recv,
    send_sem,
    recv_sem,
    fsend_sem,
    frecv_sem,
    load_sem,
):
    dom = lax.axis_index("dom")
    sub = lax.axis_index("sub")

    def out_peer(idx):
        r, t = idx // N_SUB, idx % N_SUB
        peer = dom + r - 2
        valid = (peer >= 0) & (peer < n_dom) & jnp.logical_not((r == 2) & (t == sub))
        return peer, t, valid

    def in_peer(idx):
        r, t = idx // N_SUB, idx % N_SUB
        peer = dom - r + 2
        valid = (peer >= 0) & (peer < n_dom) & jnp.logical_not((r == 2) & (t == sub))
        return peer, t, valid

    loads = [
        pltpu.make_async_copy(source, target, load_sem.at[k])
        for k, (source, target) in enumerate(
            (
                (dofs_hbm, dofs),
                (ck_hbm, ck),
                (ecl_hbm, ecl),
                (star_hbm, star),
                (stab_hbm, stab),
                (felem_hbm, felem),
                (fface_hbm, fface),
                (fcoef_hbm, fcoef),
                (ftrace_hbm, ftrace),
                (stiff_hbm, stiff),
                (lflux_hbm, lflux),
                (lsol_hbm, lsol),
                (fnbr_hbm, fnbr),
                (nface_hbm, nface),
                (flift_hbm, flift),
                (nflux_hbm, nflux),
                (nsol_hbm, nsol),
            )
        )
    ]
    for load in loads:
        load.start()
    barrier = pltpu.get_barrier_semaphore()

    @pl.loop(0, PEERS)
    def _(idx):
        peer, t, valid = out_peer(idx)

        @pl.when(valid)
        def _():
            pl.semaphore_signal(barrier, inc=1, device_id=(peer, t), device_id_type=MESH)

    lane = lax.broadcasted_iota(jnp.int32, (16, E), 1)
    low_half = lane < 64
    even = (lane // 32) % 2 == 0
    element_rows = lax.broadcasted_iota(jnp.int32, (E, E), 0)

    for load in loads[:5]:
        load.wait()
    base[...] = jnp.zeros((Q, KP, E), F32)
    base[:, :B, :] = dofs[...]
    cur[...] = base[...]
    wide[...] = jnp.zeros(wide.shape, F32)
    for d in range(3):
        wide[d, :B, :B] = ck[d]
    a_ck[...] = jnp.concatenate(
        [weights(wide[d], KP) for d in range(3)] + [jnp.zeros((8, E), F32)], axis=0
    ).astype(BF16)
    cluster_of = ecl[...]

    def star_terms(acc, coef, first, rows, group, sign):
        for q in range(Q):
            value = moved[rows : rows + KP, q * E : (q + 1) * E]
            for pp in range(3):
                term = coef[group * 3 + pp, q, first : first + 1, :] * value
                if acc[pp] is None:
                    acc[pp] = term if sign > 0 else -term
                else:
                    acc[pp] = acc[pp] + term if sign > 0 else acc[pp] - term
        return acc

    def derive(s, due):
        if s > 0:
            keep = cluster_of == 0
            if s % 2 == 0:
                keep = cluster_of <= 1
            for q in range(Q):
                base[q] = jnp.where(keep, cur[q], base[q])
        offset = jnp.where(
            cluster_of == 0, 0.0, jnp.where(cluster_of == 1, (s % 2) * STEP, (s % 4) * STEP)
        ).astype(F32)
        for c in due:
            end = offset + STEP * 2**c
            upper, lower, factor = end, offset, 1.0
            for j in range(5):
                factor = factor * (j + 1)
                wt[5 * c + j : 5 * c + j + 1, :] = (upper - lower) * (1.0 / factor)
                upper, lower = upper * end, lower * offset
        for q in range(Q):
            value = base[q]
            x_der[:, q * E : (q + 1) * E] = stacked(value)
            for c in due:
                integ[c, q] = wt[5 * c : 5 * c + 1, :] * value

        @pl.loop(0, 4)
        def _(j):
            moved[0:E, :] = dot(a_ck[...], x_der[...])

            @pl.loop(0, 3)
            def _(group):
                acc = [None, None, None]
                for d in range(3):
                    acc = star_terms(acc, star, d, d * KP, group, -1)
                for pp in range(3):
                    p = group * 3 + pp
                    x_der[:, lanes(p)] = stacked(acc[pp])
                    for c in due:
                        integ[c, p] = integ[c, p] + wt[pl.ds(5 * c + 1 + j, 1), :] * acc[pp]

    def pack(c, route, now=False):
        for q in range(Q):
            comp[32 * q : 32 * q + 32, :] = integ[c, q, 0:32, :]
        for q in range(Q):
            comp[TAIL + 3 * q : TAIL + 3 * q + 8, :] = integ[c, q, 32:40, :]
        high, low = halves(comp[...])
        comp_h[c] = jnp.concatenate([high, low], axis=1).astype(BF16)
        picks = pick_send[c]
        packed[...] = dot(comp_h[c], jnp.concatenate([picks, picks], axis=0))

        @pl.loop(0, REACH)
        def _(r):
            for chunk in range(PIECE // 16):
                parts = [
                    packed[PIECE * g + 16 * chunk : PIECE * g + 16 * chunk + 16, lanes(r)]
                    for g in range(4)
                ]
                for t, part in enumerate(exchanged(parts, low_half, even)):
                    send[route, r * N_SUB + t, 16 * chunk : 16 * chunk + 16, :] = part
            if now:
                send_block(route, r)

        recv[route, 2 * N_SUB + sub] = send[route, 2 * N_SUB + sub]

    def ghost_copy(route, out_idx, landing, peer, t):
        return pltpu.make_async_remote_copy(
            src_ref=send.at[route, out_idx],
            dst_ref=recv.at[route, landing],
            send_sem=send_sem.at[route, out_idx],
            recv_sem=recv_sem.at[route, landing],
            device_id=(peer, t),
            device_id_type=MESH,
        )

    def send_block(route, r):
        for t in range(N_SUB):
            idx = r * N_SUB + t
            peer, _, valid = out_peer(idx)

            @pl.when(valid)
            def _():
                ghost_copy(route, idx, r * N_SUB + sub, peer, t).start()

    def sent(*routes):
        for route in routes:

            @pl.loop(0, PEERS)
            def _(idx, route=route):
                peer, t, valid = out_peer(idx)

                @pl.when(valid)
                def _():
                    ghost_copy(route, idx, (idx // N_SUB) * N_SUB + sub, peer, t).wait_send()

    def local_gather(c, first):
        picks = pick[c, 0]
        value = dot(comp_h[c], jnp.concatenate([picks, picks], axis=0))
        if first:
            got[...] = value
        else:
            got[...] += value

    def ghost_gather(c, route, then=None):
        if then is not None:
            for r in range(1):
                send_block(then, r)
        @pl.loop(0, REACH)
        def _(r):
            for t in range(N_SUB):
                idx = r * N_SUB + t
                peer, _, valid = in_peer(idx)

                @pl.when(valid)
                def _():
                    ghost_copy(route, idx, idx, peer, t).wait_recv()

            if then is not None:

                @pl.when(r + 1 < REACH)
                def _():
                    send_block(then, r + 1)

            for chunk in range(PIECE // 16):
                parts = [
                    recv[route, r * N_SUB + t, 16 * chunk : 16 * chunk + 16, :]
                    for t in range(N_SUB)
                ]
                for g, part in enumerate(exchanged(parts, low_half, even)):
                    start = PIECE * g + 16 * chunk
                    high, low = halves(part)
                    ghost[start : start + 16, 0:E] = high.astype(BF16)
                    ghost[start : start + 16, E : 2 * E] = low.astype(BF16)
            picks = pick[c, 1 + r]
            got[...] += dot(ghost[...], jnp.concatenate([picks, picks], axis=0))

    def own_columns(due):
        for q in range(Q):
            own = None
            for c in due:
                part = jnp.where(cluster_of == c, integ[c, q], 0.0)
                own = part if own is None else own + part
            x_own[:, q * E : (q + 1) * E] = stacked(own)

    def far_copy(s):
        return pltpu.make_async_remote_copy(
            src_ref=fsend.at[s],
            dst_ref=frecv.at[s],
            send_sem=fsend_sem.at[s],
            recv_sem=frecv_sem.at[s],
            device_id=(dom, (sub + 2) % N_SUB),
            device_id_type=MESH,
        )

    def send_near(s):
        moved[0:64, :] = dot(a_tr[...], x_own[...])
        marks = [cfe[16:17, :] == (i + 1.0) for i in range(4)]
        for q in range(Q):
            value = jnp.zeros((16, E), F32)
            for i in range(4):
                part = moved[16 * i : 16 * i + 16, q * E : (q + 1) * E]
                value = value + jnp.where(marks[i], part, 0.0)
            near[16 * q : 16 * q + 16, :] = value
        folded = None
        for g in range(4):
            high, low = halves(near[KP * g : KP * g + KP, :])
            part = dot(jnp.concatenate([high, low], axis=0).astype(BF16), pick_f[g])
            part = part[0:KP] + part[KP : 2 * KP]
            folded = part if folded is None else folded + part
        fsend[s] = folded
        far_copy(s).start()

    def volume():
        moved[...] = dot(a_vol[...], x_own[...])

        for group in range(3):
            acc = [cur[group * 3 + pp] for pp in range(3)]
            for d in range(3):
                acc = star_terms(acc, star, d, d * KP, group, 1)
            for i in range(4):
                acc = star_terms(acc, lsol, i, (3 + i) * KP, group, -1)
            for pp in range(3):
                cur[group * 3 + pp] = acc[pp]

    def fault(s):
        far_copy(s).wait_recv()
        high, low = halves(frecv[s])
        value = jnp.concatenate([high, low], axis=0).astype(BF16)
        for g in range(4):
            part = dot(value, pick_ft[g])
            far[KP * g : KP * g + KP, :] = part[0:KP] + part[KP : 2 * KP]
        for q in range(Q):
            mine, other = near[16 * q : 16 * q + 16, :], far[16 * q : 16 * q + 16, :]
            state = 0.5 * (mine + other) + cfe[q : q + 1, :] * (other - mine)
            high, low = halves(state)
            cols = slice(q * E, (q + 1) * E)
            x_state[0:48, cols] = jnp.concatenate([high, low, high], axis=0).astype(BF16)
        lift[...] = dot(a_li[...], x_state[...])

    def neighbours():
        for i in range(4):
            for q in range(Q):
                main = got[32 * q : 32 * q + 32, i * E : (i + 1) * E]
                tail = got[TAIL + 3 * q : TAIL + 3 * q + 8, i * E : (i + 1) * E]
                x_nbr[:, q * E : (q + 1) * E] = stacked(jnp.concatenate([main, tail], axis=0))
            across[...] = dot(a_nf[i], x_nbr[...])
            which = nface[i : i + 1, :]
            mark = cfe[16:17, :] == (i + 1.0)
            at = i * KP
            for q in range(Q):
                cols = slice(q * E, (q + 1) * E)
                value = across[3 * KP : 4 * KP, cols]
                for j in range(2, -1, -1):
                    value = jnp.where(which == j, across[j * KP : (j + 1) * KP, cols], value)
                lifted[pl.ds(at, KP), cols] = value + jnp.where(mark, lift[pl.ds(at, KP), cols], 0.0)

        for group in range(3):
            acc = [cur[group * 3 + pp] for pp in range(3)]
            for i in range(4):
                for q in range(Q):
                    value = lifted[i * KP : (i + 1) * KP, q * E : (q + 1) * E]
                    for pp in range(3):
                        acc[pp] = acc[pp] - nsol[group * 3 + pp, q, i : i + 1, :] * value
            for pp in range(3):
                cur[group * 3 + pp] = acc[pp]

    def prepare_pick_send(c):
        for r in range(REACH):
            row = tab[c, r : r + 1, :]
            pick_send[c, :, r * E : (r + 1) * E] = jnp.where(element_rows == row, 1.0, 0.0).astype(BF16)

    def prepare_pick(c):
        @pl.loop(0, 1 + REACH)
        def _(g):
            for i in range(4):
                row = jnp.where(cluster_of == c, fnbr[i : i + 1, :] - E * g, -1)
                cols = slice(i * E, (i + 1) * E)
                pick[c, g, :, cols] = jnp.where(element_rows == row, 1.0, 0.0).astype(BF16)

    derive(0, (0, 1, 2))
    for c in range(3):
        for r in range(REACH):
            for t in range(N_SUB):
                tab[c, r : r + 1, SLOT * t : SLOT * (t + 1)] = stab[c, r, t : t + 1, :]
    prepare_pick_send(0)
    @pl.loop(0, REACH)
    def _(r):
        peer = dom - r + 2

        @pl.when((peer < 0) | (peer >= n_dom))
        def _():
            @pl.loop(0, len(ROUTES))
            def _(route):
                for t in range(N_SUB):
                    recv[route, r * N_SUB + t] = jnp.zeros((PIECE, E), F32)

    groups = jnp.minimum(dom + 2, n_dom - 1) - jnp.maximum(dom - 2, 0) + 1
    pl.semaphore_wait(barrier, groups * N_SUB - 1)

    pack(0, ROUTES[0, 0], True)


    for load in loads[5:9]:
        load.wait()
    own_columns((0, 1, 2))
    wide_at = 3
    for i in range(4):
        wide[wide_at + i, :FB, :B] = ftrace[:, i, :]
    a_tr[...] = jnp.concatenate(
        [weights(wide[wide_at + i, 0:16, :], KP) for i in range(4)], axis=0
    ).astype(BF16)
    wide_at += 4
    fer[...] = jnp.full(fer.shape, -1, jnp.int32)
    for g in range(4):
        fer[g : g + 1, NF * g : NF * (g + 1)] = felem[...]
    for g in range(4):
        spot = jnp.where(element_rows == fer[g : g + 1, :], 1.0, 0.0)
        pick_f[g] = spot.astype(BF16)
        pick_ft[g] = spot.T.astype(BF16)
    cfs[...] = jnp.zeros(cfs.shape, F32)
    cfs[0:Q, 0:NF] = fcoef[...]
    cfs[16:17, 0:NF] = (fface[...] + 1).astype(F32)
    high, low = halves(cfs[...])
    spread = dot(jnp.concatenate([high, low], axis=0).astype(BF16), pick_ft[0])
    cfe[...] = spread[0:32] + spread[32:64]
    near[...] = jnp.zeros(near.shape, F32)
    x_state[...] = jnp.zeros(x_state.shape, BF16)
    send_near(0)

    for c in (1, 2):
        prepare_pick_send(c)
        pack(c, ROUTES[0, c])

    for load in loads[9:]:
        load.wait()
    for d in range(3):
        wide[wide_at + d, :B, :B] = stiff[d]
    for i in range(4):
        wide[wide_at + 3 + i, :B, :B] = lflux[:, i, :]
    a_vol[...] = jnp.concatenate(
        [weights(wide[wide_at + m], KP) for m in range(7)] + [jnp.zeros((8, E), F32)], axis=0
    ).astype(BF16)
    wide_at += 7
    volume()
    prepare_pick(0)
    for i in range(4):
        for j in range(4):
            wide[wide_at + 4 * i + j, :B, :B] = nflux[i, :, j, :]
        a_nf[i] = jnp.concatenate(
            [weights(wide[wide_at + 4 * i + j], KP) for j in range(4)], axis=0
        ).astype(BF16)
    wide_at += 16
    sides_in[...] = jnp.zeros((E, E), F32)
    for i in range(4):
        sides_in[16 * i : 16 * i + FB, :B] = flift[:, i, :]
    sides = sides_in[...].T[0:KP]
    first = lax.broadcasted_iota(jnp.int32, (KP, E), 1) < 16
    parts = [jnp.where(first, pltpu.roll(sides, (E - 16 * i) % E, 1), 0.0) for i in range(4)]
    a_li[...] = jnp.concatenate([weights(part, 16) for part in parts], axis=0).astype(BF16)
    local_gather(0, True)
    fault(0)
    prepare_pick(1)
    ghost_gather(0, ROUTES[0, 0], ROUTES[0, 1])
    neighbours()

    derive(1, (0,))
    pack(0, ROUTES[1, 0], True)
    local_gather(1, True)
    own_columns((0,))
    send_near(1)
    volume()
    local_gather(0, False)
    prepare_pick(2)
    ghost_gather(1, ROUTES[0, 1])
    fault(1)
    sent(ROUTES[0, 0])
    ghost_gather(0, ROUTES[1, 0], ROUTES[0, 2])
    neighbours()

    derive(2, (0, 1))
    pack(0, ROUTES[2, 0], True)
    local_gather(2, True)
    own_columns((0, 1))
    send_near(2)
    pack(1, ROUTES[2, 1])
    volume()
    local_gather(0, False)
    ghost_gather(2, ROUTES[0, 2])
    fault(2)
    sent(ROUTES[0, 1], ROUTES[1, 0])
    ghost_gather(0, ROUTES[2, 0], ROUTES[2, 1])
    neighbours()

    derive(3, (0,))
    pack(0, ROUTES[3, 0], True)
    local_gather(1, True)
    own_columns((0,))
    send_near(3)
    volume()
    local_gather(0, False)
    ghost_gather(1, ROUTES[2, 1])
    fault(3)
    sent(ROUTES[0, 2], ROUTES[2, 0], ROUTES[2, 1])
    ghost_gather(0, ROUTES[3, 0])
    neighbours()
    out[...] = cur[:, :B, :]

    sent(ROUTES[3, 0])
    for s in range(4):
        far_copy(s).wait_send()


def body(n_dom, *args):
    args = list(args)
    for index in (4, 8, 9):
        args[index] = args[index].reshape(1, -1)
    for index, order in ((1, (1, 2, 0, 3)), (2, (1, 2, 0, 3)), (3, (1, 2, 0, 3))):
        args[index] = args[index].transpose(order)
    for index, order in ((13, (1, 0, 2)), (14, (0, 2, 1, 3)), (15, (1, 0, 2)), (16, (2, 0, 1))):
        args[index] = args[index].transpose(order)
    specs = [pl.BlockSpec(memory_space=pltpu.HBM)] * len(args)
    routes = len(ROUTES)
    scratch = [pltpu.VMEM(arg.shape, arg.dtype) for arg in args] + [
        pltpu.VMEM((Q, KP, E), F32),
        pltpu.VMEM((Q, KP, E), F32),
        pltpu.VMEM((3, Q, KP, E), F32),
        pltpu.VMEM((E, W), BF16),
        pltpu.VMEM((E, W), BF16),
        pltpu.VMEM((E, W), BF16),
        pltpu.VMEM((E, W), BF16),
        pltpu.VMEM((288, W), F32),
        pltpu.VMEM((4 * KP, W), F32),
        pltpu.VMEM((4 * KP, W), F32),
        pltpu.VMEM((4 * KP, W), F32),
        pltpu.VMEM((4 * KP, E), F32),
        pltpu.VMEM((4 * KP, E), F32),
        pltpu.VMEM((4, KP, E), F32),
        pltpu.VMEM((4, KP, E), F32),
        pltpu.VMEM((ROWS, E), F32),
        pltpu.VMEM((3, ROWS, 2 * E), BF16),
        pltpu.VMEM((ROWS, 4 * E), F32),
        pltpu.VMEM((ROWS, 2 * E), BF16),
        pltpu.VMEM((ROWS, REACH * E), F32),
        pltpu.VMEM((3, 1 + REACH, E, 4 * E), BF16),
        pltpu.VMEM((3, E, REACH * E), BF16),
        pltpu.VMEM((4, E, E), BF16),
        pltpu.VMEM((4, E, E), BF16),
        pltpu.VMEM((E, E), BF16),
        pltpu.VMEM((288, E), BF16),
        pltpu.VMEM((4, 4 * KP, E), BF16),
        pltpu.VMEM((64, E), BF16),
        pltpu.VMEM((4 * KP, E), BF16),
        pltpu.VMEM((30, KP, E), F32),
        pltpu.VMEM((E, E), F32),
        pltpu.VMEM((3, 8, E), jnp.int32),
        pltpu.VMEM((8, E), jnp.int32),
        pltpu.VMEM((32, E), F32),
        pltpu.VMEM((32, E), F32),
        pltpu.VMEM((16, E), F32),
        pltpu.VMEM((routes, PEERS, PIECE, E), F32),
        pltpu.VMEM((routes, PEERS, PIECE, E), F32),
        pltpu.SemaphoreType.DMA((routes, PEERS)),
        pltpu.SemaphoreType.DMA((routes, PEERS)),
        pltpu.SemaphoreType.DMA((4,)),
        pltpu.SemaphoreType.DMA((4,)),
        pltpu.SemaphoreType.DMA((17,)),
    ]
    return pl.pallas_call(
        functools.partial(kernel, n_dom),
        out_shape=jax.ShapeDtypeStruct((Q, B, E), F32),
        in_specs=specs,
        out_specs=pl.BlockSpec(memory_space=pltpu.VMEM),
        scratch_shapes=scratch,
        compiler_params=pltpu.CompilerParams(
            collective_id=0, has_side_effects=True, vmem_limit_bytes=60 * 1024 * 1024
        ),
    )(*args)


def solution(mesh):
    in_specs = (
        P(None, None, ("dom", "sub")),
        P(None, None, None, ("dom", "sub")),
        P(None, None, None, ("dom", "sub")),
        P(None, None, None, ("dom", "sub")),
        P(("dom", "sub")),
        P(None, ("dom", "sub")),
        P(None, ("dom", "sub")),
        P(("dom", "sub"), None, None, None),
        P(("dom", "sub")),
        P(("dom", "sub")),
        P(None, ("dom", "sub")),
        P(),
        P(),
        P(),
        P(),
        P(),
        P(),
    )
    out_specs = P(None, None, ("dom", "sub"))
    return jax.shard_map(
        functools.partial(body, mesh.shape["dom"]),
        mesh=mesh,
        in_specs=in_specs,
        out_specs=out_specs,
        check_vma=False,
    )
```

```python
import functools

import jax
import jax.numpy as jnp
from jax import lax
from jax.experimental import pallas as pl
from jax.experimental.pallas import tpu as pltpu
from jax.sharding import PartitionSpec as P

MESH = pl.DeviceIdType.MESH
F32 = jnp.float32
BF16 = jnp.bfloat16
Q = 9
B = 35
KP = 40
E = 128
W = Q * E
FB = 15
NF = 32
SLOT = 32
REACH = 5
N_SUB = 4
PEERS = REACH * N_SUB
ROWS = 320
PIECE = ROWS // N_SUB
TAIL = Q * 32
STEP = 0.25
ROUTES = {(0, 0): 0, (0, 1): 1, (0, 2): 2, (1, 0): 3, (2, 0): 4, (2, 1): 5, (3, 0): 6}


def halves(value):
    high = value.astype(BF16).astype(F32)
    return high, value - high


def stacked(value):
    high, low = halves(value)
    return jnp.concatenate([high, low, high, jnp.zeros((8, E), F32)], axis=0).astype(BF16)


def weights(matrix, width):
    high, low = halves(matrix)
    return high + pltpu.roll(high, width, 1) + pltpu.roll(low, 2 * width, 1)


def dot(left, right):
    return jnp.dot(left, right, preferred_element_type=F32)


def lanes(index, count=1):
    return pl.ds(pl.multiple_of(index * E, E), count * E)


def exchanged(parts, low_half, even):
    mixed = [None] * 4
    for g in range(2):
        mixed[g] = jnp.where(low_half, parts[g], pltpu.roll(parts[g + 2], 64, 1))
        mixed[g + 2] = jnp.where(low_half, pltpu.roll(parts[g], 64, 1), parts[g + 2])
    out = [None] * 4
    for g in (0, 2):
        out[g] = jnp.where(even, mixed[g], pltpu.roll(mixed[g + 1], 32, 1))
        out[g + 1] = jnp.where(even, pltpu.roll(mixed[g], 96, 1), mixed[g + 1])
    return out


def kernel(
    n_dom,
    dofs_hbm,
    star_hbm,
    lsol_hbm,
    nsol_hbm,
    ecl_hbm,
    fnbr_hbm,
    nface_hbm,
    stab_hbm,
    felem_hbm,
    fface_hbm,
    fcoef_hbm,
    ck_hbm,
    stiff_hbm,
    lflux_hbm,
    nflux_hbm,
    ftrace_hbm,
    flift_hbm,
    out,
    dofs,
    star,
    lsol,
    nsol,
    ecl,
    fnbr,
    nface,
    stab,
    felem,
    fface,
    fcoef,
    ck,
    stiff,
    lflux,
    nflux,
    ftrace,
    flift,
    base,
    cur,
    integ,
    x_der,
    x_own,
    x_nbr,
    x_state,
    moved,
    across,
    lifted,
    lift,
    near,
    far,
    fsend,
    frecv,
    comp,
    comp_h,
    got,
    ghost,
    packed,
    pick,
    pick_send,
    pick_f,
    pick_ft,
    a_ck,
    a_vol,
    a_nf,
    a_tr,
    a_li,
    wide,
    sides_in,
    tab,
    fer,
    cfs,
    cfe,
    wt,
    send,
    recv,
    send_sem,
    recv_sem,
    fsend_sem,
    frecv_sem,
    load_sem,
):
    dom = lax.axis_index("dom")
    sub = lax.axis_index("sub")

    def out_peer(idx):
        r, t = idx // N_SUB, idx % N_SUB
        peer = dom + r - 2
        valid = (peer >= 0) & (peer < n_dom) & jnp.logical_not((r == 2) & (t == sub))
        return peer, t, valid

    def in_peer(idx):
        r, t = idx // N_SUB, idx % N_SUB
        peer = dom - r + 2
        valid = (peer >= 0) & (peer < n_dom) & jnp.logical_not((r == 2) & (t == sub))
        return peer, t, valid

    loads = [
        pltpu.make_async_copy(source, target, load_sem.at[k])
        for k, (source, target) in enumerate(
            (
                (dofs_hbm, dofs),
                (ck_hbm, ck),
                (ecl_hbm, ecl),
                (star_hbm, star),
                (stab_hbm, stab),
                (felem_hbm, felem),
                (fface_hbm, fface),
                (fcoef_hbm, fcoef),
                (ftrace_hbm, ftrace),
                (stiff_hbm, stiff),
                (lflux_hbm, lflux),
                (lsol_hbm, lsol),
                (fnbr_hbm, fnbr),
                (nface_hbm, nface),
                (flift_hbm, flift),
                (nflux_hbm, nflux),
                (nsol_hbm, nsol),
            )
        )
    ]
    for load in loads:
        load.start()
    barrier = pltpu.get_barrier_semaphore()

    @pl.loop(0, PEERS)
    def _(idx):
        peer, t, valid = out_peer(idx)

        @pl.when(valid)
        def _():
            pl.semaphore_signal(barrier, inc=1, device_id=(peer, t), device_id_type=MESH)

    lane = lax.broadcasted_iota(jnp.int32, (16, E), 1)
    low_half = lane < 64
    even = (lane // 32) % 2 == 0
    element_rows = lax.broadcasted_iota(jnp.int32, (E, E), 0)

    for load in loads[:5]:
        load.wait()
    base[...] = jnp.zeros((Q, KP, E), F32)
    base[:, :B, :] = dofs[...]
    cur[...] = base[...]
    wide[...] = jnp.zeros(wide.shape, F32)
    for d in range(3):
        wide[d, :B, :B] = ck[d]
    a_ck[...] = jnp.concatenate(
        [weights(wide[d], KP) for d in range(3)] + [jnp.zeros((8, E), F32)], axis=0
    ).astype(BF16)
    cluster_of = ecl[...]

    def star_terms(acc, coef, first, rows, group, sign):
        for q in range(Q):
            value = moved[rows : rows + KP, q * E : (q + 1) * E]
            for pp in range(3):
                term = coef[group * 3 + pp, q, first : first + 1, :] * value
                if acc[pp] is None:
                    acc[pp] = term if sign > 0 else -term
                else:
                    acc[pp] = acc[pp] + term if sign > 0 else acc[pp] - term
        return acc

    def derive(s, due):
        if s > 0:
            keep = cluster_of == 0
            if s % 2 == 0:
                keep = cluster_of <= 1
            for q in range(Q):
                base[q] = jnp.where(keep, cur[q], base[q])
        offset = jnp.where(
            cluster_of == 0, 0.0, jnp.where(cluster_of == 1, (s % 2) * STEP, (s % 4) * STEP)
        ).astype(F32)
        for c in due:
            end = offset + STEP * 2**c
            upper, lower, factor = end, offset, 1.0
            for j in range(5):
                factor = factor * (j + 1)
                wt[5 * c + j : 5 * c + j + 1, :] = (upper - lower) * (1.0 / factor)
                upper, lower = upper * end, lower * offset
        for q in range(Q):
            value = base[q]
            x_der[:, q * E : (q + 1) * E] = stacked(value)
            for c in due:
                integ[c, q] = wt[5 * c : 5 * c + 1, :] * value

        @pl.loop(0, 4)
        def _(j):
            moved[0:E, :] = dot(a_ck[...], x_der[...])

            @pl.loop(0, 3)
            def _(group):
                acc = [None, None, None]
                for d in range(3):
                    acc = star_terms(acc, star, d, d * KP, group, -1)
                for pp in range(3):
                    p = group * 3 + pp
                    x_der[:, lanes(p)] = stacked(acc[pp])
                    for c in due:
                        integ[c, p] = integ[c, p] + wt[pl.ds(5 * c + 1 + j, 1), :] * acc[pp]

    def pack(c, route, now=False):
        for q in range(Q):
            comp[32 * q : 32 * q + 32, :] = integ[c, q, 0:32, :]
        for q in range(Q):
            comp[TAIL + 3 * q : TAIL + 3 * q + 8, :] = integ[c, q, 32:40, :]
        high, low = halves(comp[...])
        comp_h[c] = jnp.concatenate([high, low], axis=1).astype(BF16)
        picks = pick_send[c]
        packed[...] = dot(comp_h[c], jnp.concatenate([picks, picks], axis=0))

        @pl.loop(0, REACH)
        def _(r):
            for chunk in range(PIECE // 16):
                parts = [
                    packed[PIECE * g + 16 * chunk : PIECE * g + 16 * chunk + 16, lanes(r)]
                    for g in range(4)
                ]
                for t, part in enumerate(exchanged(parts, low_half, even)):
                    send[route, r * N_SUB + t, 16 * chunk : 16 * chunk + 16, :] = part
            if now:
                send_block(route, r)

        recv[route, 2 * N_SUB + sub] = send[route, 2 * N_SUB + sub]

    def ghost_copy(route, out_idx, landing, peer, t):
        return pltpu.make_async_remote_copy(
            src_ref=send.at[route, out_idx],
            dst_ref=recv.at[route, landing],
            send_sem=send_sem.at[route, out_idx],
            recv_sem=recv_sem.at[route, landing],
            device_id=(peer, t),
            device_id_type=MESH,
        )

    def send_block(route, r):
        for turn in (2, 1, 3, 0):
            t = (sub + turn) % N_SUB
            idx = r * N_SUB + t
            peer, _, valid = out_peer(idx)

            @pl.when(valid)
            def _():
                ghost_copy(route, idx, r * N_SUB + sub, peer, t).start()

    def sent(*routes):
        for route in routes:

            @pl.loop(0, PEERS)
            def _(idx, route=route):
                peer, t, valid = out_peer(idx)

                @pl.when(valid)
                def _():
                    ghost_copy(route, idx, (idx // N_SUB) * N_SUB + sub, peer, t).wait_send()

    def local_gather(c, first):
        picks = pick[c, 0]
        value = dot(comp_h[c], jnp.concatenate([picks, picks], axis=0))
        if first:
            got[...] = value
        else:
            got[...] += value

    def ghost_gather(c, route, then=None):
        if then is not None:
            for r in range(1):
                send_block(then, r)
        @pl.loop(0, REACH)
        def _(r):
            for t in range(N_SUB):
                idx = r * N_SUB + t
                peer, _, valid = in_peer(idx)

                @pl.when(valid)
                def _():
                    ghost_copy(route, idx, idx, peer, t).wait_recv()

            if then is not None:

                @pl.when(r + 1 < REACH)
                def _():
                    send_block(then, r + 1)

            for chunk in range(PIECE // 16):
                parts = [
                    recv[route, r * N_SUB + t, 16 * chunk : 16 * chunk + 16, :]
                    for t in range(N_SUB)
                ]
                for g, part in enumerate(exchanged(parts, low_half, even)):
                    start = PIECE * g + 16 * chunk
                    high, low = halves(part)
                    ghost[start : start + 16, 0:E] = high.astype(BF16)
                    ghost[start : start + 16, E : 2 * E] = low.astype(BF16)
            picks = pick[c, 1 + r]
            got[...] += dot(ghost[...], jnp.concatenate([picks, picks], axis=0))

    def own_columns(due):
        for q in range(Q):
            own = None
            for c in due:
                part = jnp.where(cluster_of == c, integ[c, q], 0.0)
                own = part if own is None else own + part
            x_own[:, q * E : (q + 1) * E] = stacked(own)

    def far_copy(s):
        return pltpu.make_async_remote_copy(
            src_ref=fsend.at[s],
            dst_ref=frecv.at[s],
            send_sem=fsend_sem.at[s],
            recv_sem=frecv_sem.at[s],
            device_id=(dom, (sub + 2) % N_SUB),
            device_id_type=MESH,
        )

    def send_near(s):
        moved[0:64, :] = dot(a_tr[...], x_own[...])
        marks = [cfe[16:17, :] == (i + 1.0) for i in range(4)]
        for q in range(Q):
            value = jnp.zeros((16, E), F32)
            for i in range(4):
                part = moved[16 * i : 16 * i + 16, q * E : (q + 1) * E]
                value = value + jnp.where(marks[i], part, 0.0)
            near[16 * q : 16 * q + 16, :] = value
        folded = None
        for g in range(4):
            high, low = halves(near[KP * g : KP * g + KP, :])
            part = dot(jnp.concatenate([high, low], axis=0).astype(BF16), pick_f[g])
            part = part[0:KP] + part[KP : 2 * KP]
            folded = part if folded is None else folded + part
        fsend[s] = folded
        far_copy(s).start()

    def volume():
        moved[...] = dot(a_vol[...], x_own[...])

        for group in range(3):
            acc = [cur[group * 3 + pp] for pp in range(3)]
            for d in range(3):
                acc = star_terms(acc, star, d, d * KP, group, 1)
            for i in range(4):
                acc = star_terms(acc, lsol, i, (3 + i) * KP, group, -1)
            for pp in range(3):
                cur[group * 3 + pp] = acc[pp]

    def fault(s):
        far_copy(s).wait_recv()
        high, low = halves(frecv[s])
        value = jnp.concatenate([high, low], axis=0).astype(BF16)
        for g in range(4):
            part = dot(value, pick_ft[g])
            far[KP * g : KP * g + KP, :] = part[0:KP] + part[KP : 2 * KP]
        for q in range(Q):
            mine, other = near[16 * q : 16 * q + 16, :], far[16 * q : 16 * q + 16, :]
            state = 0.5 * (mine + other) + cfe[q : q + 1, :] * (other - mine)
            high, low = halves(state)
            cols = slice(q * E, (q + 1) * E)
            x_state[0:48, cols] = jnp.concatenate([high, low, high], axis=0).astype(BF16)
        lift[...] = dot(a_li[...], x_state[...])

    def neighbours():
        for i in range(4):
            for q in range(Q):
                main = got[32 * q : 32 * q + 32, i * E : (i + 1) * E]
                tail = got[TAIL + 3 * q : TAIL + 3 * q + 8, i * E : (i + 1) * E]
                x_nbr[:, q * E : (q + 1) * E] = stacked(jnp.concatenate([main, tail], axis=0))
            across[...] = dot(a_nf[i], x_nbr[...])
            which = nface[i : i + 1, :]
            mark = cfe[16:17, :] == (i + 1.0)
            at = i * KP
            for q in range(Q):
                cols = slice(q * E, (q + 1) * E)
                value = across[3 * KP : 4 * KP, cols]
                for j in range(2, -1, -1):
                    value = jnp.where(which == j, across[j * KP : (j + 1) * KP, cols], value)
                lifted[pl.ds(at, KP), cols] = value + jnp.where(mark, lift[pl.ds(at, KP), cols], 0.0)

        for group in range(3):
            acc = [cur[group * 3 + pp] for pp in range(3)]
            for i in range(4):
                for q in range(Q):
                    value = lifted[i * KP : (i + 1) * KP, q * E : (q + 1) * E]
                    for pp in range(3):
                        acc[pp] = acc[pp] - nsol[group * 3 + pp, q, i : i + 1, :] * value
            for pp in range(3):
                cur[group * 3 + pp] = acc[pp]

    def prepare_pick_send(c):
        for r in range(REACH):
            row = tab[c, r : r + 1, :]
            pick_send[c, :, r * E : (r + 1) * E] = jnp.where(element_rows == row, 1.0, 0.0).astype(BF16)

    def prepare_pick(c):
        @pl.loop(0, 1 + REACH)
        def _(g):
            for i in range(4):
                row = jnp.where(cluster_of == c, fnbr[i : i + 1, :] - E * g, -1)
                cols = slice(i * E, (i + 1) * E)
                pick[c, g, :, cols] = jnp.where(element_rows == row, 1.0, 0.0).astype(BF16)

    derive(0, (0, 1, 2))
    for c in range(3):
        for r in range(REACH):
            for t in range(N_SUB):
                tab[c, r : r + 1, SLOT * t : SLOT * (t + 1)] = stab[c, r, t : t + 1, :]
    prepare_pick_send(0)
    @pl.loop(0, REACH)
    def _(r):
        peer = dom - r + 2

        @pl.when((peer < 0) | (peer >= n_dom))
        def _():
            @pl.loop(0, len(ROUTES))
            def _(route):
                for t in range(N_SUB):
                    recv[route, r * N_SUB + t] = jnp.zeros((PIECE, E), F32)

    groups = jnp.minimum(dom + 2, n_dom - 1) - jnp.maximum(dom - 2, 0) + 1
    pl.semaphore_wait(barrier, groups * N_SUB - 1)

    pack(0, ROUTES[0, 0], True)


    for load in loads[5:9]:
        load.wait()
    own_columns((0, 1, 2))
    wide_at = 3
    for i in range(4):
        wide[wide_at + i, :FB, :B] = ftrace[:, i, :]
    a_tr[...] = jnp.concatenate(
        [weights(wide[wide_at + i, 0:16, :], KP) for i in range(4)], axis=0
    ).astype(BF16)
    wide_at += 4
    fer[...] = jnp.full(fer.shape, -1, jnp.int32)
    for g in range(4):
        fer[g : g + 1, NF * g : NF * (g + 1)] = felem[...]
    for g in range(4):
        spot = jnp.where(element_rows == fer[g : g + 1, :], 1.0, 0.0)
        pick_f[g] = spot.astype(BF16)
        pick_ft[g] = spot.T.astype(BF16)
    cfs[...] = jnp.zeros(cfs.shape, F32)
    cfs[0:Q, 0:NF] = fcoef[...]
    cfs[16:17, 0:NF] = (fface[...] + 1).astype(F32)
    high, low = halves(cfs[...])
    spread = dot(jnp.concatenate([high, low], axis=0).astype(BF16), pick_ft[0])
    cfe[...] = spread[0:32] + spread[32:64]
    near[...] = jnp.zeros(near.shape, F32)
    x_state[...] = jnp.zeros(x_state.shape, BF16)
    send_near(0)

    for c in (1, 2):
        prepare_pick_send(c)
        pack(c, ROUTES[0, c])

    for load in loads[9:]:
        load.wait()
    for d in range(3):
        wide[wide_at + d, :B, :B] = stiff[d]
    for i in range(4):
        wide[wide_at + 3 + i, :B, :B] = lflux[:, i, :]
    a_vol[...] = jnp.concatenate(
        [weights(wide[wide_at + m], KP) for m in range(7)] + [jnp.zeros((8, E), F32)], axis=0
    ).astype(BF16)
    wide_at += 7
    volume()
    prepare_pick(0)
    for i in range(4):
        for j in range(4):
            wide[wide_at + 4 * i + j, :B, :B] = nflux[i, :, j, :]
        a_nf[i] = jnp.concatenate(
            [weights(wide[wide_at + 4 * i + j], KP) for j in range(4)], axis=0
        ).astype(BF16)
    wide_at += 16
    sides_in[...] = jnp.zeros((E, E), F32)
    for i in range(4):
        sides_in[16 * i : 16 * i + FB, :B] = flift[:, i, :]
    sides = sides_in[...].T[0:KP]
    first = lax.broadcasted_iota(jnp.int32, (KP, E), 1) < 16
    parts = [jnp.where(first, pltpu.roll(sides, (E - 16 * i) % E, 1), 0.0) for i in range(4)]
    a_li[...] = jnp.concatenate([weights(part, 16) for part in parts], axis=0).astype(BF16)
    local_gather(0, True)
    fault(0)
    prepare_pick(1)
    ghost_gather(0, ROUTES[0, 0], ROUTES[0, 1])
    neighbours()

    derive(1, (0,))
    pack(0, ROUTES[1, 0], True)
    local_gather(1, True)
    own_columns((0,))
    send_near(1)
    volume()
    local_gather(0, False)
    prepare_pick(2)
    ghost_gather(1, ROUTES[0, 1])
    fault(1)
    sent(ROUTES[0, 0])
    ghost_gather(0, ROUTES[1, 0], ROUTES[0, 2])
    neighbours()

    derive(2, (0, 1))
    pack(0, ROUTES[2, 0], True)
    local_gather(2, True)
    own_columns((0, 1))
    send_near(2)
    pack(1, ROUTES[2, 1])
    volume()
    local_gather(0, False)
    ghost_gather(2, ROUTES[0, 2])
    fault(2)
    sent(ROUTES[0, 1], ROUTES[1, 0])
    ghost_gather(0, ROUTES[2, 0], ROUTES[2, 1])
    neighbours()

    derive(3, (0,))
    pack(0, ROUTES[3, 0], True)
    local_gather(1, True)
    own_columns((0,))
    send_near(3)
    volume()
    local_gather(0, False)
    ghost_gather(1, ROUTES[2, 1])
    fault(3)
    sent(ROUTES[0, 2], ROUTES[2, 0], ROUTES[2, 1])
    ghost_gather(0, ROUTES[3, 0])
    neighbours()
    out[...] = cur[:, :B, :]

    sent(ROUTES[3, 0])
    for s in range(4):
        far_copy(s).wait_send()


def body(n_dom, *args):
    args = list(args)
    for index in (4, 8, 9):
        args[index] = args[index].reshape(1, -1)
    for index, order in ((1, (1, 2, 0, 3)), (2, (1, 2, 0, 3)), (3, (1, 2, 0, 3))):
        args[index] = args[index].transpose(order)
    for index, order in ((13, (1, 0, 2)), (14, (0, 2, 1, 3)), (15, (1, 0, 2)), (16, (2, 0, 1))):
        args[index] = args[index].transpose(order)
    specs = [pl.BlockSpec(memory_space=pltpu.HBM)] * len(args)
    routes = len(ROUTES)
    scratch = [pltpu.VMEM(arg.shape, arg.dtype) for arg in args] + [
        pltpu.VMEM((Q, KP, E), F32),
        pltpu.VMEM((Q, KP, E), F32),
        pltpu.VMEM((3, Q, KP, E), F32),
        pltpu.VMEM((E, W), BF16),
        pltpu.VMEM((E, W), BF16),
        pltpu.VMEM((E, W), BF16),
        pltpu.VMEM((E, W), BF16),
        pltpu.VMEM((288, W), F32),
        pltpu.VMEM((4 * KP, W), F32),
        pltpu.VMEM((4 * KP, W), F32),
        pltpu.VMEM((4 * KP, W), F32),
        pltpu.VMEM((4 * KP, E), F32),
        pltpu.VMEM((4 * KP, E), F32),
        pltpu.VMEM((4, KP, E), F32),
        pltpu.VMEM((4, KP, E), F32),
        pltpu.VMEM((ROWS, E), F32),
        pltpu.VMEM((3, ROWS, 2 * E), BF16),
        pltpu.VMEM((ROWS, 4 * E), F32),
        pltpu.VMEM((ROWS, 2 * E), BF16),
        pltpu.VMEM((ROWS, REACH * E), F32),
        pltpu.VMEM((3, 1 + REACH, E, 4 * E), BF16),
        pltpu.VMEM((3, E, REACH * E), BF16),
        pltpu.VMEM((4, E, E), BF16),
        pltpu.VMEM((4, E, E), BF16),
        pltpu.VMEM((E, E), BF16),
        pltpu.VMEM((288, E), BF16),
        pltpu.VMEM((4, 4 * KP, E), BF16),
        pltpu.VMEM((64, E), BF16),
        pltpu.VMEM((4 * KP, E), BF16),
        pltpu.VMEM((30, KP, E), F32),
        pltpu.VMEM((E, E), F32),
        pltpu.VMEM((3, 8, E), jnp.int32),
        pltpu.VMEM((8, E), jnp.int32),
        pltpu.VMEM((32, E), F32),
        pltpu.VMEM((32, E), F32),
        pltpu.VMEM((16, E), F32),
        pltpu.VMEM((routes, PEERS, PIECE, E), F32),
        pltpu.VMEM((routes, PEERS, PIECE, E), F32),
        pltpu.SemaphoreType.DMA((routes, PEERS)),
        pltpu.SemaphoreType.DMA((routes, PEERS)),
        pltpu.SemaphoreType.DMA((4,)),
        pltpu.SemaphoreType.DMA((4,)),
        pltpu.SemaphoreType.DMA((17,)),
    ]
    return pl.pallas_call(
        functools.partial(kernel, n_dom),
        out_shape=jax.ShapeDtypeStruct((Q, B, E), F32),
        in_specs=specs,
        out_specs=pl.BlockSpec(memory_space=pltpu.VMEM),
        scratch_shapes=scratch,
        compiler_params=pltpu.CompilerParams(
            collective_id=0, has_side_effects=True, vmem_limit_bytes=60 * 1024 * 1024
        ),
    )(*args)


def solution(mesh):
    in_specs = (
        P(None, None, ("dom", "sub")),
        P(None, None, None, ("dom", "sub")),
        P(None, None, None, ("dom", "sub")),
        P(None, None, None, ("dom", "sub")),
        P(("dom", "sub")),
        P(None, ("dom", "sub")),
        P(None, ("dom", "sub")),
        P(("dom", "sub"), None, None, None),
        P(("dom", "sub")),
        P(("dom", "sub")),
        P(None, ("dom", "sub")),
        P(),
        P(),
        P(),
        P(),
        P(),
        P(),
    )
    out_specs = P(None, None, ("dom", "sub"))
    return jax.shard_map(
        functools.partial(body, mesh.shape["dom"]),
        mesh=mesh,
        in_specs=in_specs,
        out_specs=out_specs,
        check_vma=False,
    )
```

```python
import functools

import jax
import jax.numpy as jnp
from jax import lax
from jax.experimental import pallas as pl
from jax.experimental.pallas import tpu as pltpu
from jax.sharding import PartitionSpec as P

MESH = pl.DeviceIdType.MESH
F32 = jnp.float32
BF16 = jnp.bfloat16
Q = 9
B = 35
KP = 40
E = 128
W = Q * E
FB = 15
NF = 32
SLOT = 32
REACH = 5
N_SUB = 4
PEERS = REACH * N_SUB
ROWS = 320
PIECE = ROWS // N_SUB
TAIL = Q * 32
STEP = 0.25
ROUTES = {(0, 0): 0, (0, 1): 1, (0, 2): 2, (1, 0): 3, (2, 0): 4, (2, 1): 5, (3, 0): 6}


def halves(value):
    high = value.astype(BF16).astype(F32)
    return high, value - high


def stacked(value):
    high, low = halves(value)
    return jnp.concatenate([high, low, high, jnp.zeros((8, E), F32)], axis=0).astype(BF16)


def weights(matrix, width):
    high, low = halves(matrix)
    return high + pltpu.roll(high, width, 1) + pltpu.roll(low, 2 * width, 1)


def dot(left, right):
    return jnp.dot(left, right, preferred_element_type=F32)


def lanes(index, count=1):
    return pl.ds(pl.multiple_of(index * E, E), count * E)


def exchanged(parts, low_half, even):
    mixed = [None] * 4
    for g in range(2):
        mixed[g] = jnp.where(low_half, parts[g], pltpu.roll(parts[g + 2], 64, 1))
        mixed[g + 2] = jnp.where(low_half, pltpu.roll(parts[g], 64, 1), parts[g + 2])
    out = [None] * 4
    for g in (0, 2):
        out[g] = jnp.where(even, mixed[g], pltpu.roll(mixed[g + 1], 32, 1))
        out[g + 1] = jnp.where(even, pltpu.roll(mixed[g], 96, 1), mixed[g + 1])
    return out


def kernel(
    n_dom,
    dofs_hbm,
    star_hbm,
    lsol_hbm,
    nsol_hbm,
    ecl_hbm,
    fnbr_hbm,
    nface_hbm,
    stab_hbm,
    felem_hbm,
    fface_hbm,
    fcoef_hbm,
    ck_hbm,
    stiff_hbm,
    lflux_hbm,
    nflux_hbm,
    ftrace_hbm,
    flift_hbm,
    out,
    dofs,
    star,
    lsol,
    nsol,
    ecl,
    fnbr,
    nface,
    stab,
    felem,
    fface,
    fcoef,
    ck,
    stiff,
    lflux,
    nflux,
    ftrace,
    flift,
    base,
    cur,
    integ,
    x_der,
    x_own,
    x_nbr,
    x_state,
    moved,
    across,
    lifted,
    lift,
    near,
    far,
    fsend,
    frecv,
    comp,
    comp_h,
    got,
    ghost,
    packed,
    pick,
    pick_send,
    pick_f,
    pick_ft,
    a_ck,
    a_vol,
    a_nf,
    a_tr,
    a_li,
    wide,
    sides_in,
    tab,
    fer,
    cfs,
    cfe,
    wt,
    send,
    recv,
    send_sem,
    recv_sem,
    fsend_sem,
    frecv_sem,
    load_sem,
):
    dom = lax.axis_index("dom")
    sub = lax.axis_index("sub")

    def out_peer(idx):
        r, t = idx // N_SUB, idx % N_SUB
        peer = dom + r - 2
        valid = (peer >= 0) & (peer < n_dom) & jnp.logical_not((r == 2) & (t == sub))
        return peer, t, valid

    def in_peer(idx):
        r, t = idx // N_SUB, idx % N_SUB
        peer = dom - r + 2
        valid = (peer >= 0) & (peer < n_dom) & jnp.logical_not((r == 2) & (t == sub))
        return peer, t, valid

    loads = [
        pltpu.make_async_copy(source, target, load_sem.at[k])
        for k, (source, target) in enumerate(
            (
                (dofs_hbm, dofs),
                (ck_hbm, ck),
                (ecl_hbm, ecl),
                (star_hbm, star),
                (stab_hbm, stab),
                (felem_hbm, felem),
                (fface_hbm, fface),
                (fcoef_hbm, fcoef),
                (ftrace_hbm, ftrace),
                (stiff_hbm, stiff),
                (lflux_hbm, lflux),
                (lsol_hbm, lsol),
                (fnbr_hbm, fnbr),
                (nface_hbm, nface),
                (flift_hbm, flift),
                (nflux_hbm, nflux),
                (nsol_hbm, nsol),
            )
        )
    ]
    for load in loads:
        load.start()
    barrier = pltpu.get_barrier_semaphore()

    @pl.loop(0, PEERS)
    def _(idx):
        peer, t, valid = out_peer(idx)

        @pl.when(valid)
        def _():
            pl.semaphore_signal(barrier, inc=1, device_id=(peer, t), device_id_type=MESH)

    lane = lax.broadcasted_iota(jnp.int32, (16, E), 1)
    low_half = lane < 64
    even = (lane // 32) % 2 == 0
    element_rows = lax.broadcasted_iota(jnp.int32, (E, E), 0)

    for load in loads[:5]:
        load.wait()
    base[...] = jnp.zeros((Q, KP, E), F32)
    base[:, :B, :] = dofs[...]
    cur[...] = base[...]
    wide[...] = jnp.zeros(wide.shape, F32)
    for d in range(3):
        wide[d, :B, :B] = ck[d]
    a_ck[...] = jnp.concatenate(
        [weights(wide[d], KP) for d in range(3)] + [jnp.zeros((8, E), F32)], axis=0
    ).astype(BF16)
    cluster_of = ecl[...]

    def star_terms(acc, coef, first, rows, group, sign):
        for q in range(Q):
            value = moved[rows : rows + KP, q * E : (q + 1) * E]
            for pp in range(3):
                term = coef[group * 3 + pp, q, first : first + 1, :] * value
                if acc[pp] is None:
                    acc[pp] = term if sign > 0 else -term
                else:
                    acc[pp] = acc[pp] + term if sign > 0 else acc[pp] - term
        return acc

    def derive(s, due):
        if s > 0:
            keep = cluster_of == 0
            if s % 2 == 0:
                keep = cluster_of <= 1
            for q in range(Q):
                base[q] = jnp.where(keep, cur[q], base[q])
        offset = jnp.where(
            cluster_of == 0, 0.0, jnp.where(cluster_of == 1, (s % 2) * STEP, (s % 4) * STEP)
        ).astype(F32)
        for c in due:
            end = offset + STEP * 2**c
            upper, lower, factor = end, offset, 1.0
            for j in range(5):
                factor = factor * (j + 1)
                wt[5 * c + j : 5 * c + j + 1, :] = (upper - lower) * (1.0 / factor)
                upper, lower = upper * end, lower * offset
        for q in range(Q):
            value = base[q]
            x_der[:, q * E : (q + 1) * E] = stacked(value)
            for c in due:
                integ[c, q] = wt[5 * c : 5 * c + 1, :] * value

        @pl.loop(0, 4)
        def _(j):
            moved[0:E, :] = dot(a_ck[...], x_der[...])

            @pl.loop(0, 3)
            def _(group):
                acc = [None, None, None]
                for d in range(3):
                    acc = star_terms(acc, star, d, d * KP, group, -1)
                for pp in range(3):
                    p = group * 3 + pp
                    x_der[:, lanes(p)] = stacked(acc[pp])
                    for c in due:
                        integ[c, p] = integ[c, p] + wt[pl.ds(5 * c + 1 + j, 1), :] * acc[pp]

    def pack(c, route, now=False):
        for q in range(Q):
            comp[32 * q : 32 * q + 32, :] = integ[c, q, 0:32, :]
        for q in range(Q):
            comp[TAIL + 3 * q : TAIL + 3 * q + 8, :] = integ[c, q, 32:40, :]
        high, low = halves(comp[...])
        comp_h[c] = jnp.concatenate([high, low], axis=1).astype(BF16)
        picks = pick_send[c]
        packed[...] = dot(comp_h[c], jnp.concatenate([picks, picks], axis=0))

        @pl.loop(0, REACH)
        def _(b):
            r = turned(b)
            for chunk in range(PIECE // 16):
                parts = [
                    packed[PIECE * g + 16 * chunk : PIECE * g + 16 * chunk + 16, lanes(r)]
                    for g in range(4)
                ]
                for t, part in enumerate(exchanged(parts, low_half, even)):
                    send[route, r * N_SUB + t, 16 * chunk : 16 * chunk + 16, :] = part
            if now:
                send_block(route, r)

        recv[route, 2 * N_SUB + sub] = send[route, 2 * N_SUB + sub]

    def turned(b):
        near_first = REACH - 1 - b
        return jnp.where(near_first % 2 == 0, near_first // 2, REACH - 1 - near_first // 2)

    def ghost_copy(route, out_idx, landing, peer, t):
        return pltpu.make_async_remote_copy(
            src_ref=send.at[route, out_idx],
            dst_ref=recv.at[route, landing],
            send_sem=send_sem.at[route, out_idx],
            recv_sem=recv_sem.at[route, landing],
            device_id=(peer, t),
            device_id_type=MESH,
        )

    def send_block(route, r):
        for turn in (2, 1, 3, 0):
            t = (sub + turn) % N_SUB
            idx = r * N_SUB + t
            peer, _, valid = out_peer(idx)

            @pl.when(valid)
            def _():
                ghost_copy(route, idx, r * N_SUB + sub, peer, t).start()

    def sent(*routes):
        for route in routes:

            @pl.loop(0, PEERS)
            def _(idx, route=route):
                peer, t, valid = out_peer(idx)

                @pl.when(valid)
                def _():
                    ghost_copy(route, idx, (idx // N_SUB) * N_SUB + sub, peer, t).wait_send()

    def local_gather(c, first):
        picks = pick[c, 0]
        value = dot(comp_h[c], jnp.concatenate([picks, picks], axis=0))
        if first:
            got[...] = value
        else:
            got[...] += value

    def ghost_gather(c, route, then=None):
        if then is not None:
            send_block(then, 2)
        @pl.loop(0, REACH)
        def _(b):
            r = turned(b)
            for t in range(N_SUB):
                idx = r * N_SUB + t
                peer, _, valid = in_peer(idx)

                @pl.when(valid)
                def _():
                    ghost_copy(route, idx, idx, peer, t).wait_recv()

            if then is not None:

                @pl.when(b + 1 < REACH)
                def _():
                    send_block(then, turned(b + 1))

            for chunk in range(PIECE // 16):
                parts = [
                    recv[route, r * N_SUB + t, 16 * chunk : 16 * chunk + 16, :]
                    for t in range(N_SUB)
                ]
                for g, part in enumerate(exchanged(parts, low_half, even)):
                    start = PIECE * g + 16 * chunk
                    high, low = halves(part)
                    ghost[start : start + 16, 0:E] = high.astype(BF16)
                    ghost[start : start + 16, E : 2 * E] = low.astype(BF16)
            picks = pick[c, 1 + r]
            got[...] += dot(ghost[...], jnp.concatenate([picks, picks], axis=0))

    def own_columns(due):
        for q in range(Q):
            own = None
            for c in due:
                part = jnp.where(cluster_of == c, integ[c, q], 0.0)
                own = part if own is None else own + part
            x_own[:, q * E : (q + 1) * E] = stacked(own)

    def far_copy(s):
        return pltpu.make_async_remote_copy(
            src_ref=fsend.at[s],
            dst_ref=frecv.at[s],
            send_sem=fsend_sem.at[s],
            recv_sem=frecv_sem.at[s],
            device_id=(dom, (sub + 2) % N_SUB),
            device_id_type=MESH,
        )

    def send_near(s):
        moved[0:64, :] = dot(a_tr[...], x_own[...])
        marks = [cfe[16:17, :] == (i + 1.0) for i in range(4)]
        for q in range(Q):
            value = jnp.zeros((16, E), F32)
            for i in range(4):
                part = moved[16 * i : 16 * i + 16, q * E : (q + 1) * E]
                value = value + jnp.where(marks[i], part, 0.0)
            near[16 * q : 16 * q + 16, :] = value
        folded = None
        for g in range(4):
            high, low = halves(near[KP * g : KP * g + KP, :])
            part = dot(jnp.concatenate([high, low], axis=0).astype(BF16), pick_f[g])
            part = part[0:KP] + part[KP : 2 * KP]
            folded = part if folded is None else folded + part
        fsend[s] = folded
        far_copy(s).start()

    def volume():
        moved[...] = dot(a_vol[...], x_own[...])

        for group in range(3):
            acc = [cur[group * 3 + pp] for pp in range(3)]
            for d in range(3):
                acc = star_terms(acc, star, d, d * KP, group, 1)
            for i in range(4):
                acc = star_terms(acc, lsol, i, (3 + i) * KP, group, -1)
            for pp in range(3):
                cur[group * 3 + pp] = acc[pp]

    def fault(s):
        far_copy(s).wait_recv()
        high, low = halves(frecv[s])
        value = jnp.concatenate([high, low], axis=0).astype(BF16)
        for g in range(4):
            part = dot(value, pick_ft[g])
            far[KP * g : KP * g + KP, :] = part[0:KP] + part[KP : 2 * KP]
        for q in range(Q):
            mine, other = near[16 * q : 16 * q + 16, :], far[16 * q : 16 * q + 16, :]
            state = 0.5 * (mine + other) + cfe[q : q + 1, :] * (other - mine)
            high, low = halves(state)
            cols = slice(q * E, (q + 1) * E)
            x_state[0:48, cols] = jnp.concatenate([high, low, high], axis=0).astype(BF16)
        lift[...] = dot(a_li[...], x_state[...])

    def neighbours():
        for i in range(4):
            for q in range(Q):
                main = got[32 * q : 32 * q + 32, i * E : (i + 1) * E]
                tail = got[TAIL + 3 * q : TAIL + 3 * q + 8, i * E : (i + 1) * E]
                x_nbr[:, q * E : (q + 1) * E] = stacked(jnp.concatenate([main, tail], axis=0))
            across[...] = dot(a_nf[i], x_nbr[...])
            which = nface[i : i + 1, :]
            mark = cfe[16:17, :] == (i + 1.0)
            at = i * KP
            for q in range(Q):
                cols = slice(q * E, (q + 1) * E)
                value = across[3 * KP : 4 * KP, cols]
                for j in range(2, -1, -1):
                    value = jnp.where(which == j, across[j * KP : (j + 1) * KP, cols], value)
                lifted[pl.ds(at, KP), cols] = value + jnp.where(mark, lift[pl.ds(at, KP), cols], 0.0)

        for group in range(3):
            acc = [cur[group * 3 + pp] for pp in range(3)]
            for i in range(4):
                for q in range(Q):
                    value = lifted[i * KP : (i + 1) * KP, q * E : (q + 1) * E]
                    for pp in range(3):
                        acc[pp] = acc[pp] - nsol[group * 3 + pp, q, i : i + 1, :] * value
            for pp in range(3):
                cur[group * 3 + pp] = acc[pp]

    def prepare_pick_send(c):
        for r in range(REACH):
            row = tab[c, r : r + 1, :]
            pick_send[c, :, r * E : (r + 1) * E] = jnp.where(element_rows == row, 1.0, 0.0).astype(BF16)

    def prepare_pick(c):
        @pl.loop(0, 1 + REACH)
        def _(g):
            for i in range(4):
                row = jnp.where(cluster_of == c, fnbr[i : i + 1, :] - E * g, -1)
                cols = slice(i * E, (i + 1) * E)
                pick[c, g, :, cols] = jnp.where(element_rows == row, 1.0, 0.0).astype(BF16)

    derive(0, (0, 1, 2))
    for c in range(3):
        for r in range(REACH):
            for t in range(N_SUB):
                tab[c, r : r + 1, SLOT * t : SLOT * (t + 1)] = stab[c, r, t : t + 1, :]
    prepare_pick_send(0)
    @pl.loop(0, REACH)
    def _(r):
        peer = dom - r + 2

        @pl.when((peer < 0) | (peer >= n_dom))
        def _():
            @pl.loop(0, len(ROUTES))
            def _(route):
                for t in range(N_SUB):
                    recv[route, r * N_SUB + t] = jnp.zeros((PIECE, E), F32)

    groups = jnp.minimum(dom + 2, n_dom - 1) - jnp.maximum(dom - 2, 0) + 1
    pl.semaphore_wait(barrier, groups * N_SUB - 1)

    pack(0, ROUTES[0, 0], True)


    for load in loads[5:9]:
        load.wait()
    own_columns((0, 1, 2))
    wide_at = 3
    for i in range(4):
        wide[wide_at + i, :FB, :B] = ftrace[:, i, :]
    a_tr[...] = jnp.concatenate(
        [weights(wide[wide_at + i, 0:16, :], KP) for i in range(4)], axis=0
    ).astype(BF16)
    wide_at += 4
    fer[...] = jnp.full(fer.shape, -1, jnp.int32)
    for g in range(4):
        fer[g : g + 1, NF * g : NF * (g + 1)] = felem[...]
    for g in range(4):
        spot = jnp.where(element_rows == fer[g : g + 1, :], 1.0, 0.0)
        pick_f[g] = spot.astype(BF16)
        pick_ft[g] = spot.T.astype(BF16)
    cfs[...] = jnp.zeros(cfs.shape, F32)
    cfs[0:Q, 0:NF] = fcoef[...]
    cfs[16:17, 0:NF] = (fface[...] + 1).astype(F32)
    high, low = halves(cfs[...])
    spread = dot(jnp.concatenate([high, low], axis=0).astype(BF16), pick_ft[0])
    cfe[...] = spread[0:32] + spread[32:64]
    near[...] = jnp.zeros(near.shape, F32)
    x_state[...] = jnp.zeros(x_state.shape, BF16)
    send_near(0)

    for c in (1, 2):
        prepare_pick_send(c)
        pack(c, ROUTES[0, c])

    for load in loads[9:]:
        load.wait()
    for d in range(3):
        wide[wide_at + d, :B, :B] = stiff[d]
    for i in range(4):
        wide[wide_at + 3 + i, :B, :B] = lflux[:, i, :]
    a_vol[...] = jnp.concatenate(
        [weights(wide[wide_at + m], KP) for m in range(7)] + [jnp.zeros((8, E), F32)], axis=0
    ).astype(BF16)
    wide_at += 7
    volume()
    prepare_pick(0)
    for i in range(4):
        for j in range(4):
            wide[wide_at + 4 * i + j, :B, :B] = nflux[i, :, j, :]
        a_nf[i] = jnp.concatenate(
            [weights(wide[wide_at + 4 * i + j], KP) for j in range(4)], axis=0
        ).astype(BF16)
    wide_at += 16
    sides_in[...] = jnp.zeros((E, E), F32)
    for i in range(4):
        sides_in[16 * i : 16 * i + FB, :B] = flift[:, i, :]
    sides = sides_in[...].T[0:KP]
    first = lax.broadcasted_iota(jnp.int32, (KP, E), 1) < 16
    parts = [jnp.where(first, pltpu.roll(sides, (E - 16 * i) % E, 1), 0.0) for i in range(4)]
    a_li[...] = jnp.concatenate([weights(part, 16) for part in parts], axis=0).astype(BF16)
    local_gather(0, True)
    fault(0)
    prepare_pick(1)
    ghost_gather(0, ROUTES[0, 0], ROUTES[0, 1])
    neighbours()

    derive(1, (0,))
    pack(0, ROUTES[1, 0], True)
    local_gather(1, True)
    own_columns((0,))
    send_near(1)
    volume()
    local_gather(0, False)
    prepare_pick(2)
    ghost_gather(1, ROUTES[0, 1])
    fault(1)
    sent(ROUTES[0, 0])
    ghost_gather(0, ROUTES[1, 0], ROUTES[0, 2])
    neighbours()

    derive(2, (0, 1))
    pack(0, ROUTES[2, 0], True)
    local_gather(2, True)
    own_columns((0, 1))
    send_near(2)
    pack(1, ROUTES[2, 1])
    volume()
    local_gather(0, False)
    ghost_gather(2, ROUTES[0, 2])
    fault(2)
    sent(ROUTES[0, 1], ROUTES[1, 0])
    ghost_gather(0, ROUTES[2, 0], ROUTES[2, 1])
    neighbours()

    derive(3, (0,))
    pack(0, ROUTES[3, 0], True)
    local_gather(1, True)
    own_columns((0,))
    send_near(3)
    volume()
    local_gather(0, False)
    ghost_gather(1, ROUTES[2, 1])
    fault(3)
    sent(ROUTES[0, 2], ROUTES[2, 0], ROUTES[2, 1])
    ghost_gather(0, ROUTES[3, 0])
    neighbours()
    out[...] = cur[:, :B, :]

    sent(ROUTES[3, 0])
    for s in range(4):
        far_copy(s).wait_send()


def body(n_dom, *args):
    args = list(args)
    for index in (4, 8, 9):
        args[index] = args[index].reshape(1, -1)
    for index, order in ((1, (1, 2, 0, 3)), (2, (1, 2, 0, 3)), (3, (1, 2, 0, 3))):
        args[index] = args[index].transpose(order)
    for index, order in ((13, (1, 0, 2)), (14, (0, 2, 1, 3)), (15, (1, 0, 2)), (16, (2, 0, 1))):
        args[index] = args[index].transpose(order)
    specs = [pl.BlockSpec(memory_space=pltpu.HBM)] * len(args)
    routes = len(ROUTES)
    scratch = [pltpu.VMEM(arg.shape, arg.dtype) for arg in args] + [
        pltpu.VMEM((Q, KP, E), F32),
        pltpu.VMEM((Q, KP, E), F32),
        pltpu.VMEM((3, Q, KP, E), F32),
        pltpu.VMEM((E, W), BF16),
        pltpu.VMEM((E, W), BF16),
        pltpu.VMEM((E, W), BF16),
        pltpu.VMEM((E, W), BF16),
        pltpu.VMEM((288, W), F32),
        pltpu.VMEM((4 * KP, W), F32),
        pltpu.VMEM((4 * KP, W), F32),
        pltpu.VMEM((4 * KP, W), F32),
        pltpu.VMEM((4 * KP, E), F32),
        pltpu.VMEM((4 * KP, E), F32),
        pltpu.VMEM((4, KP, E), F32),
        pltpu.VMEM((4, KP, E), F32),
        pltpu.VMEM((ROWS, E), F32),
        pltpu.VMEM((3, ROWS, 2 * E), BF16),
        pltpu.VMEM((ROWS, 4 * E), F32),
        pltpu.VMEM((ROWS, 2 * E), BF16),
        pltpu.VMEM((ROWS, REACH * E), F32),
        pltpu.VMEM((3, 1 + REACH, E, 4 * E), BF16),
        pltpu.VMEM((3, E, REACH * E), BF16),
        pltpu.VMEM((4, E, E), BF16),
        pltpu.VMEM((4, E, E), BF16),
        pltpu.VMEM((E, E), BF16),
        pltpu.VMEM((288, E), BF16),
        pltpu.VMEM((4, 4 * KP, E), BF16),
        pltpu.VMEM((64, E), BF16),
        pltpu.VMEM((4 * KP, E), BF16),
        pltpu.VMEM((30, KP, E), F32),
        pltpu.VMEM((E, E), F32),
        pltpu.VMEM((3, 8, E), jnp.int32),
        pltpu.VMEM((8, E), jnp.int32),
        pltpu.VMEM((32, E), F32),
        pltpu.VMEM((32, E), F32),
        pltpu.VMEM((16, E), F32),
        pltpu.VMEM((routes, PEERS, PIECE, E), F32),
        pltpu.VMEM((routes, PEERS, PIECE, E), F32),
        pltpu.SemaphoreType.DMA((routes, PEERS)),
        pltpu.SemaphoreType.DMA((routes, PEERS)),
        pltpu.SemaphoreType.DMA((4,)),
        pltpu.SemaphoreType.DMA((4,)),
        pltpu.SemaphoreType.DMA((17,)),
    ]
    return pl.pallas_call(
        functools.partial(kernel, n_dom),
        out_shape=jax.ShapeDtypeStruct((Q, B, E), F32),
        in_specs=specs,
        out_specs=pl.BlockSpec(memory_space=pltpu.VMEM),
        scratch_shapes=scratch,
        compiler_params=pltpu.CompilerParams(
            collective_id=0, has_side_effects=True, vmem_limit_bytes=60 * 1024 * 1024
        ),
    )(*args)


def solution(mesh):
    in_specs = (
        P(None, None, ("dom", "sub")),
        P(None, None, None, ("dom", "sub")),
        P(None, None, None, ("dom", "sub")),
        P(None, None, None, ("dom", "sub")),
        P(("dom", "sub")),
        P(None, ("dom", "sub")),
        P(None, ("dom", "sub")),
        P(("dom", "sub"), None, None, None),
        P(("dom", "sub")),
        P(("dom", "sub")),
        P(None, ("dom", "sub")),
        P(),
        P(),
        P(),
        P(),
        P(),
        P(),
    )
    out_specs = P(None, None, ("dom", "sub"))
    return jax.shard_map(
        functools.partial(body, mesh.shape["dom"]),
        mesh=mesh,
        in_specs=in_specs,
        out_specs=out_specs,
        check_vma=False,
    )
```
